128 devices in a mesh: dom: 32 (over x, y, core), sub: 4 (over z).
Axes of the slice: x: 4, y: 4, z: 4, core: 2. Of those that a mesh axis runs over, the one named last changes fastest.
Arguments:
- positions: float32 [3, 16384, 128], P(None, ('dom', 'sub')), may hold values from -1 to 1
- masses: float32 [16384, 128], P(('dom', 'sub')), may hold values from 0.0002 to 0.002
- counts: int32 [16384], P(('dom', 'sub')), may hold values from 1 to 128
- export_block: int32 [32768], P(('dom', 'sub')), may hold values from 0 to 127
- export_dest: int32 [32768, 1], P(('dom', 'sub')), may hold values from 0 to 127; in each aligned block of 256 rows (0 to 255, 256 to 511, ...) at most 4 rows name the same one
- near_pairs: int32 [131072, 2], P(('dom', 'sub')), may hold values from 0 to 639, as said below
- node_of_block: int32 [16384], P(('dom', 'sub')), may hold values from 0 to 2047
- far_nodes: int32 [16384, 32], P(('dom', 'sub')), may hold values from 0 to 2047
- far_offset: int32 [16384, 32], P(('dom', 'sub')), may hold values from 0 to 15
- node_centers: float32 [3, 2048], replicated, may hold values from -0.5 to 0.5
- m2l_ops: float32 [16, 84, 84], replicated, may hold values from -0.125 to 0.125
Outputs:
- field: float32 [4, 16384, 128], P(None, ('dom', 'sub'))
The draws below stay inside these ranges and needn't reach their ends.
Inputs may be any that keep to these rules, and one draw needn't show every extreme that they name: Each block's first counts slots hold live particles. `export_dest`: at most 4 rows of one device name the same destination, and some device sends exactly 4 copies to one destination. `near_pairs`: the first column is a local block below 128, the second a pool index below 640 never equal to the first.
All inputs are finite; a program needn't handle non-finite values.
Results may differ from the reference program's by a relative error of at most 0.0003.
Values sent between devices are 32-bit elements; how exact they have to be, the bound alone decides.
No kernel may reach another device: no remote copies, remote signals or barrier semaphores. Data moves between devices by JAX's collectives and lax.ppermute only.
A program may use at most 64 MiB of HBM per device.

```python
import math
import jax
import jax.numpy as jnp
import numpy as np
from jax import lax

BLOCK_PARTICLES = 128
NCOEF = 84
NBD = 128
TOP = 2048
NFAR = 32
NOFF = 16
DEVICE_TOTAL = 128
BLOCKS = 16384
EXPORT_COPIES = 256
SEND_LIMIT = 4
POOL = 640
NPAIR = 1024


def draw_near_pairs(key, part):
    key = jax.random.fold_in(key, 11)
    first_key, second_key = jax.random.split(key)
    target = jax.random.randint(first_key, (DEVICE_TOTAL * NPAIR,), 0, NBD)
    source = jax.random.randint(second_key, (DEVICE_TOTAL * NPAIR,), 0, POOL)
    source = jnp.where(source == target, (target + 1) % NBD, source)
    return jnp.stack([target, source], 1).astype(jnp.int32)


def place_ends(entries, stream_key, low, high):
    longest = entries.shape.index(max(entries.shape))
    spots = []
    for shift in (0, 1):
        where = [jax.random.randint(jax.random.fold_in(stream_key, axis), (), 0, length) for axis, length in enumerate(entries.shape)]
        where[longest] = (where[longest] + shift) % entries.shape[longest]
        spots.append(tuple(where))
    return entries.at[spots[0]].set(low).at[spots[1]].set(high)


def block_scale(rng, dims, cuts, low, largest):
    def one(axis_at, parts):
        steps = jax.random.uniform(jax.random.fold_in(jax.random.fold_in(rng, 6), axis_at), (parts,), jnp.float32, low / len(cuts), largest / len(cuts))
        return jnp.repeat(jnp.exp(steps), dims[axis_at] // parts).reshape((-1,) + (1,) * (len(dims) - axis_at - 1))

    gain = one(*cuts[0])
    for cut in cuts[1:]:
        gain = gain * one(*cut)
    return gain


def deal_out(own_key, own, number, rows, amount, top, most, skew):
    order = jax.random.permutation(own_key, amount)
    crowded, usual = shares(amount, rows * top, most, skew, True), shares(amount, rows * top, most, skew, False)
    places = jnp.arange(amount)

    def named(lengths, offset_by):
        used = int((lengths > 0).sum())
        fixed = max(1, used // 4)
        moved = fixed + (places - fixed + offset_by * (used - fixed)) % max(1, amount - fixed)
        return jnp.zeros((amount,), jnp.int32).at[order[jnp.where(places < fixed, places, moved)]].set(jnp.asarray(lengths, jnp.int32))

    lengths = jnp.where(number % 4 == 0, named(crowded, number // 4), named(usual, number - number // 4 - 1))
    mixed = jax.random.permutation(jax.random.fold_in(own, 3), amount)
    giver, taker = mixed[0:amount // 2 * 2:2], mixed[1:amount // 2 * 2:2]
    slack = jnp.minimum(lengths[giver] - 1, most - lengths[taker]) // 2
    slack = jnp.where((giver == order[0]) | (taker == order[0]) | (lengths[taker] == 0), 0, jnp.maximum(slack, 0))
    moved = jax.random.randint(jax.random.fold_in(own, 4), (amount // 2,), 0, 1 << 20) % (slack + 1)
    lengths = lengths.at[giver].add(-moved).at[taker].add(moved)
    items = jnp.searchsorted(jnp.cumsum(lengths), jnp.arange(rows * top), side="right").astype(jnp.int32)
    table = items.reshape(top, rows).T
    table = table[jax.random.permutation(jax.random.fold_in(own, 1), rows)]
    offset_by = jax.random.randint(jax.random.fold_in(own, 2), (rows, 1), 0, top)
    return jnp.take_along_axis(table, (jnp.arange(top)[None, :] + offset_by) % top, axis=1)


def shares(amount, total, most, lean, full):
    weights = [(1 << 20) // math.isqrt(standing ** lean) + 1 for standing in range(1, amount + 1)]
    largest = most if full else min(most, max(-(-total // amount), total * weights[0] // sum(weights)))
    least = 1 if total - largest >= amount - 1 else 0
    given, spare = [largest] + [least] * (amount - 1), total - largest - least * (amount - 1)
    while spare > 0:
        free = [i for i in range(1, amount) if given[i] < largest] or [i for i in range(1, amount) if given[i] < most]
        whole, budget = sum([weights[i] for i in free]), spare
        for i in free:
            extra = min(most - given[i], max(1, budget * weights[i] // whole), spare)
            given[i] = given[i] + extra
            spare = spare - extra
    return np.array(given)


def scatter_about(stream_key, shape, deviation, limit, held_as=jnp.bfloat16):
    return jnp.clip(deviation * jax.random.normal(stream_key, shape, jnp.float32), -limit, limit).astype(held_as)


def setup_inputs(seed: int = 0) -> dict:
    keys = jax.random.split(jax.random.key(seed), 12)
    positions = jnp.clip(jax.random.uniform(keys[0], (3, BLOCKS, BLOCK_PARTICLES), jnp.float32, -1.0, 1.0) * block_scale(keys[0], (3, BLOCKS, BLOCK_PARTICLES), ((1, 128),), -0.4, 0.0), -1.0, 1.0)
    masses = jnp.clip(jnp.exp(math.log(0.002) - 2.3025852 * jax.random.uniform(keys[1], (BLOCKS, BLOCK_PARTICLES), jnp.float32) ** block_scale(keys[1], (BLOCKS, BLOCK_PARTICLES), ((0, 128),), -0.2, 0.2)), 0.0002, 0.002)
    counts = place_ends(jax.random.randint(keys[2], (BLOCKS,), 1, BLOCK_PARTICLES + 1), jax.random.fold_in(keys[2], 1), 1, BLOCK_PARTICLES).astype(jnp.int32)
    export_block = place_ends(jax.random.randint(keys[3], (DEVICE_TOTAL * EXPORT_COPIES,), 0, NBD), jax.random.fold_in(keys[3], 1), 0, NBD - 1).astype(jnp.int32)
    export_dest_keys = jax.random.split(jax.random.fold_in(keys[4], 1), (DEVICE_TOTAL * EXPORT_COPIES) // EXPORT_COPIES)
    export_dest_turns = jax.random.permutation(jax.random.fold_in(keys[4], 3), (DEVICE_TOTAL * EXPORT_COPIES) // EXPORT_COPIES)
    export_dest = jax.vmap(lambda own, number: deal_out(jax.random.fold_in(keys[4], 2), own, number, EXPORT_COPIES, DEVICE_TOTAL, 1, SEND_LIMIT, 2))(export_dest_keys, export_dest_turns).reshape((DEVICE_TOTAL * EXPORT_COPIES, 1))
    near_pairs = draw_near_pairs(jax.random.fold_in(keys[11], 71), 0)
    node_of_block = place_ends(jax.random.randint(keys[6], (BLOCKS,), 0, TOP), jax.random.fold_in(keys[6], 1), 0, TOP - 1).astype(jnp.int32)
    far_nodes = place_ends(jax.random.randint(keys[7], (BLOCKS, NFAR), 0, TOP), jax.random.fold_in(keys[7], 1), 0, TOP - 1).astype(jnp.int32)
    far_offset = place_ends(jax.random.randint(keys[8], (BLOCKS, NFAR), 0, NOFF), jax.random.fold_in(keys[8], 1), 0, NOFF - 1).astype(jnp.int32)
    node_centers = jnp.clip(jax.random.uniform(keys[9], (3, TOP), jnp.float32, -0.5, 0.5), -0.5, 0.5)
    m2l_ops = scatter_about(keys[10], (NOFF, NCOEF, NCOEF), (NCOEF * NFAR) ** -0.5, 0.125, jnp.float32)
    return {"positions": positions, "masses": masses, "counts": counts, "export_block": export_block, "export_dest": export_dest, "near_pairs": near_pairs, "node_of_block": node_of_block, "far_nodes": far_nodes, "far_offset": far_offset, "node_centers": node_centers, "m2l_ops": m2l_ops}


SOFTENING = 0.0025
MAXIMAL_ORDER = lax.Precision.HIGHEST

def exponent_table():
    triples = []
    for degree in range(7):
        for first in range(degree, -1, -1):
            for second in range(degree - first, -1, -1):
                triples.append((first, second, degree - first - second))
    return triples

def gradient_tables():
    triples = exponent_table()
    lookup = {}
    for place, triple in enumerate(triples):
        lookup[triple] = place
    tables = np.zeros((4, len(triples), len(triples)), np.float32)
    tables[0] = np.eye(len(triples), dtype=np.float32)
    for place, triple in enumerate(triples):
        for axis in range(3):
            if triple[axis] > 0:
                lower = list(triple)
                lower[axis] -= 1
                tables[axis + 1, place, lookup[tuple(lower)]] = -float(triple[axis])
    return tables

def monomials(offset):
    powers = []
    for axis in range(3):
        column = [jnp.ones_like(offset[axis])]
        for order in range(6):
            column.append(column[-1] * offset[axis])
        powers.append(column)
    return jnp.stack([powers[0][one] * powers[1][two] * powers[2][three] for one, two, three in exponent_table()])

def pair_terms(target_block, source_block):
    delta = [source_block[axis][None, :] - target_block[axis][:, None] for axis in range(3)]
    dist2 = delta[0] * delta[0] + delta[1] * delta[1] + delta[2] * delta[2] + SOFTENING
    inverse = lax.rsqrt(dist2)
    cubed = inverse * inverse * inverse
    source_mass = source_block[3][None, :]
    target_mass = target_block[3][:, None]
    on_target = [-lax.optimization_barrier(jnp.sum(source_mass * inverse, 1))] + [lax.optimization_barrier(jnp.sum(source_mass * delta[axis] * cubed, 1)) for axis in range(3)]
    on_source = [-lax.optimization_barrier(jnp.sum(target_mass * inverse, 0))] + [-lax.optimization_barrier(jnp.sum(target_mass * delta[axis] * cubed, 0)) for axis in range(3)]
    return (jnp.stack(on_target), jnp.stack(on_source))

def reference(positions, masses, counts, export_block, export_dest, near_pairs, node_of_block, far_nodes, far_offset, node_centers, m2l_ops):
    tables = jnp.asarray(gradient_tables())
    slots = jnp.arange(BLOCK_PARTICLES)
    live = slots[None, :] < counts[:, None]
    weights = jnp.where(live, masses, jnp.float32(0.0))
    blocks = jnp.concatenate([jnp.transpose(positions, (1, 0, 2)), weights[:, None, :]], 1)
    centers = jnp.transpose(node_centers[:, node_of_block])
    blocks_dev = blocks.reshape(DEVICE_TOTAL, NBD, 4, BLOCK_PARTICLES)
    centers_dev = centers.reshape(DEVICE_TOTAL, NBD, 3)

    def block_moments(inputs):
        own, own_centers = inputs
        monomial_terms = monomials(jnp.transpose(own[:, :3, :], (1, 0, 2)) - jnp.transpose(own_centers)[:, :, None])
        return jnp.einsum('kbp,bp->bk', monomial_terms, own[:, 3, :], precision=MAXIMAL_ORDER)
    per_block = lax.map(block_moments, (blocks_dev, centers_dev))
    moments = jax.ops.segment_sum(per_block.reshape(DEVICE_TOTAL * NBD, NCOEF), node_of_block, num_segments=TOP)
    dest = export_dest[:, 0].reshape(DEVICE_TOTAL, EXPORT_COPIES)
    chosen = export_block.reshape(DEVICE_TOTAL, EXPORT_COPIES)
    order = jnp.arange(EXPORT_COPIES)
    earlier = (dest[:, :, None] == dest[:, None, :]) & (order[None, None, :] < order[None, :, None])
    rank = lax.optimization_barrier(jnp.sum(earlier.astype(jnp.int32), 2))
    owner_rows = (jnp.arange(DEVICE_TOTAL)[:, None] * NBD + chosen).astype(jnp.int32)
    particle_rows = blocks[owner_rows.reshape(-1)].reshape(DEVICE_TOTAL, EXPORT_COPIES, 4 * BLOCK_PARTICLES)

    def visit(field, inputs):
        device, own, own_centers, pairs, own_far_nodes, own_far_offset = inputs
        selection_mask = ((dest == device)[:, None, :] & (rank[:, None, :] == jnp.arange(SEND_LIMIT)[None, :, None])).astype(jnp.float32)
        inbound_blocks = jnp.einsum('evi,eix->evx', selection_mask, particle_rows, precision=MAXIMAL_ORDER).reshape(DEVICE_TOTAL * SEND_LIMIT, 4, BLOCK_PARTICLES)
        pool = jnp.concatenate([own, inbound_blocks], 0)

        def one_pair(pair):
            return pair_terms(pool[pair[0]], pool[pair[1]])
        target_terms, source_terms = lax.map(one_pair, pairs, batch_size=16)
        pool_field = jax.ops.segment_sum(source_terms, pairs[:, 1], num_segments=NBD + DEVICE_TOTAL * SEND_LIMIT)
        near = jax.ops.segment_sum(target_terms, pairs[:, 0], num_segments=NBD) + pool_field[:NBD]
        reaction_forces = pool_field[NBD:].reshape(DEVICE_TOTAL, SEND_LIMIT, 4 * BLOCK_PARTICLES)
        returned_rows = jnp.einsum('lsn,lsx->lnx', selection_mask, reaction_forces, precision=MAXIMAL_ORDER).reshape(DEVICE_TOTAL * EXPORT_COPIES, 4, BLOCK_PARTICLES)
        field = field.at[owner_rows.reshape(-1)].add(returned_rows)
        monomial_terms = monomials(jnp.transpose(own[:, :3, :], (1, 0, 2)) - jnp.transpose(own_centers)[:, :, None])
        gathered = moments[own_far_nodes]
        local_exp = jnp.einsum('bjlk,bjk->bl', m2l_ops[own_far_offset], gathered, precision=MAXIMAL_ORDER)
        series_coefficients = jnp.einsum('bk,gkl->bgl', local_exp, tables, precision=MAXIMAL_ORDER)
        distant_field = jnp.einsum('bgl,lbp->bgp', series_coefficients, monomial_terms, precision=MAXIMAL_ORDER)
        start = (device * NBD).astype(jnp.int32)
        current = lax.dynamic_slice_in_dim(field, start, NBD, 0)
        field = lax.dynamic_update_slice_in_dim(field, current + near + distant_field, start, 0)
        return (field, None)
    devices = jnp.arange(DEVICE_TOTAL).astype(jnp.int32)
    start_field = jnp.zeros((DEVICE_TOTAL * NBD, 4, BLOCK_PARTICLES), jnp.float32)
    inputs = (devices, blocks_dev, centers_dev, near_pairs.reshape(DEVICE_TOTAL, NPAIR, 2), far_nodes.reshape(DEVICE_TOTAL, NBD, NFAR), far_offset.reshape(DEVICE_TOTAL, NBD, NFAR))
    field, unused = lax.scan(visit, start_field, inputs)
    field = jnp.where(live[:, None, :], field, jnp.float32(0.0))
    return jnp.transpose(field, (1, 0, 2))
```

```python
import jax
import jax.numpy as jnp
import numpy as np
from jax import lax
from jax.experimental import pallas as pl
from jax.experimental.pallas import tpu as pltpu
from jax.sharding import PartitionSpec as P

SOFTENING = 0.0025
LANES = 128
NBLK = 128
NDEV = 128
SLOTS = 4
NNODE = 2048
NROWS = 256
NPAIRS = 1024
NFAR = 32
NOFF = 16
NCOEF = 84
INBOUND = NDEV * SLOTS
POOL = NBLK + INBOUND
NBUCKET = 8
AXES = ("dom", "sub")
VMEM_LIMIT = 56 * 1024 * 1024
F32 = jnp.float32
I32 = jnp.int32


def exponent_table():
    triples = []
    for degree in range(7):
        for first in range(degree, -1, -1):
            for second in range(degree - first, -1, -1):
                triples.append((first, second, degree - first - second))
    return triples


TRIPLES = exponent_table()
PLACE = {triple: place for place, triple in enumerate(TRIPLES)}


def monomial_chain(root, x, y, z):
    terms = []
    for a, b, c in TRIPLES:
        if a > 0:
            lower, axis = (a - 1, b, c), x
        elif b > 0:
            lower, axis = (a, b - 1, c), y
        elif c > 0:
            lower, axis = (a, b, c - 1), z
        else:
            terms.append(root)
            continue
        parent = terms[PLACE[lower]]
        terms.append(axis if parent is None else parent * axis)
    return terms


def prep_kernel(
    block_s, dest_s, node_s, pos, mass, counts, nodes, centers,
    local, outgoing, partial, slots, offsets, mom, used,
):
    lane = lax.broadcasted_iota(I32, (8, LANES), 1)
    sub = lax.broadcasted_iota(I32, (8, LANES), 0)
    wide = lax.broadcasted_iota(I32, (8, NNODE), 1).astype(F32)
    counts_row = counts[...].astype(F32)
    nodes_row = nodes[...].astype(F32)

    def group(g, carry):
        rows = pl.ds(pl.multiple_of(g * 8, 8), 8)
        diag = lane == sub + 8 * g
        count_col = jnp.sum(jnp.where(diag, counts_row, 0.0), 1, keepdims=True)
        node_col = jnp.sum(jnp.where(diag, nodes_row, 0.0), 1, keepdims=True)
        weight = jnp.where(lane.astype(F32) < count_col, mass[rows, :], 0.0)
        picked = wide == node_col
        rel = []
        for axis in range(3):
            center = jnp.sum(
                jnp.where(picked, centers[axis : axis + 1, :], 0.0), 1, keepdims=True
            )
            here = pos[axis, rows, :]
            local[pl.ds(32 * g + axis, 8, stride=4), :] = here
            rel.append(here - center)
            offsets[axis, rows, :] = rel[axis]
        local[pl.ds(32 * g + 3, 8, stride=4), :] = weight
        terms = monomial_chain(weight, *rel)
        total = jnp.zeros((8, LANES), F32)
        for k in range(NCOEF):
            total = jnp.where(lane == k, jnp.sum(terms[k], 1, keepdims=True), total)
        mom[rows, :] = total
        return carry

    lax.fori_loop(0, NBLK // 8, group, 0)
    partial[...] = jnp.zeros_like(partial)
    outgoing[...] = jnp.zeros_like(outgoing)

    def bin_block(b, carry):
        n = node_s[b]
        partial[pl.ds(n, 1), :] = partial[pl.ds(n, 1), :] + mom[pl.ds(b, 1), :]
        return carry

    lax.fori_loop(0, NBLK, bin_block, 0, unroll=8)

    def clear(i, carry):
        used[i] = 0
        return carry

    lax.fori_loop(0, NDEV, clear, 0, unroll=8)

    def place(r, carry):
        d = dest_s[r]
        k = used[d]
        used[d] = k + 1
        s = d * SLOTS + k
        slots[r] = s
        outgoing[pl.ds(4 * s, 4), :] = local[pl.ds(4 * block_s[r], 4), :]
        return carry

    lax.fori_loop(0, NROWS, place, 0, unroll=8)


GANG = 2
ORDER = NPAIRS + NBLK * (GANG - 1)
CHUNKS = NBLK // 32
POOL_ROWS = 4 * POOL + 8


def build_kernel(inbound, counts, pairs, meta):
    wide_sub = lax.broadcasted_iota(I32, (8, NPAIRS), 0)
    counts_row = counts[...].astype(F32)
    lane = lax.broadcasted_iota(I32, (8, LANES), 1)
    sub = lax.broadcasted_iota(I32, (8, LANES), 0)
    square_lane = lax.broadcasted_iota(I32, (LANES, LANES), 1)
    square_sub = lax.broadcasted_iota(I32, (LANES, LANES), 0)
    target = pairs[0:1, :]
    source = pairs[1:2, :]

    def received(g, total):
        weight = inbound[pl.ds(32 * g + 3, 8, stride=4), :]
        col = jnp.sum(jnp.where(weight > 0.0, 1.0, 0.0), 1, keepdims=True)
        return total + jnp.where(wide_sub + 8 * g + NBLK == source, col, 0.0)

    live = lax.fori_loop(0, INBOUND // 8, received, jnp.zeros((8, NPAIRS), F32))
    live = jnp.sum(live, 0, keepdims=True)
    live = jnp.logical_or(live > 0.0, source < NBLK)
    goal = jnp.where(live, target, -1)
    totals = jnp.zeros((LANES, LANES), F32)
    for c in range(NPAIRS // LANES):
        totals = totals + (square_sub == goal[:, c * LANES : (c + 1) * LANES]).astype(F32)
    totals = jnp.sum(totals, 1, keepdims=True)
    gangs = jnp.floor((totals + (GANG - 1)) * (1.0 / GANG))
    diag = square_lane == square_sub
    gangs_row = jnp.sum(jnp.where(diag, gangs, 0.0), 0, keepdims=True)
    starts = jnp.sum(jnp.where(square_lane < square_sub, gangs_row * GANG, 0.0), 1, keepdims=True)
    starts_row = jnp.sum(jnp.where(diag, starts, 0.0), 0, keepdims=True)
    upper = (square_sub < square_lane).astype(F32)
    running = starts
    for c in range(NPAIRS // LANES):
        part = goal[:, c * LANES : (c + 1) * LANES]
        hit = (square_sub == part).astype(F32)
        ahead = jnp.dot(hit, upper, preferred_element_type=F32) + running
        place = jnp.sum(hit * ahead, 0, keepdims=True)
        place = jnp.where(part < 0, float(ORDER), place).astype(I32)
        meta[0:1, c * LANES : (c + 1) * LANES] = place
        running = running + jnp.sum(hit, 1, keepdims=True)
    meta[1:2, :] = source
    meta[2:8, :] = jnp.zeros((6, NPAIRS), I32)
    meta[2:3, 0:LANES] = starts_row.astype(I32)
    meta[3:4, 0:LANES] = gangs_row.astype(I32)


def near_kernel(
    meta, counts, local, inbound, near_local, near_inbound,
    pool, turned, acc_t, acc_c, rows_s, sums_s, order,
):
    pool[pl.ds(0, 4 * NBLK), :] = local[...]
    pool[pl.ds(4 * NBLK, 4 * INBOUND), :] = inbound[...]
    pool[pl.ds(4 * POOL, 8), :] = jnp.zeros((8, LANES), F32)
    for c in range(CHUNKS):
        turned[c] = local[c * 128 : c * 128 + 128, :].T
        acc_t[c] = jnp.zeros((128, LANES), F32)

    def zero(c, carry):
        acc_c[pl.ds(pl.multiple_of(c * 128, 128), 128), :] = jnp.zeros((128, LANES), F32)
        return carry

    lax.fori_loop(0, (POOL + 4) * 32 // 128, zero, 0)

    def clear(i, carry):
        order[i] = POOL
        return carry

    lax.fori_loop(0, ORDER, clear, 0, unroll=8)

    def scatter(p, carry):
        order[meta[0, p]] = meta[1, p]
        return carry

    lax.fori_loop(0, NPAIRS, scatter, 0, unroll=8)
    lane = lax.broadcasted_iota(I32, (8, LANES), 1)

    def run(level, t):
        chunk = lax.shift_right_logical(t, 5)
        first = lax.bitwise_and(t, 31) * 4
        picks = [jnp.zeros((8, LANES), I32) + (first + comp) for comp in range(4)]
        masks = [lane == pick for pick in picks]
        for k in range(2 * level):
            view = turned[chunk, 8 * k : 8 * k + 8, :]
            for comp in range(4):
                rows_s[4 * k + comp] = jnp.take_along_axis(view, picks[comp], axis=1)
                sums_s[4 * k + comp] = jnp.zeros((8, LANES), F32)
        base = meta[2, t]

        def step(i, carry):
            places, cols, sums = [], [], []
            for u in range(GANG):
                col = order[base + i * GANG + u]
                places.append(col)
                cols.append(
                    [
                        jnp.broadcast_to(pool[pl.ds(4 * col + comp, 1), :], (8, LANES))
                        for comp in range(4)
                    ]
                )
                sums.append([jnp.zeros((8, LANES), F32)] * 4)
            for k in range(2 * level):
                rows = [rows_s[4 * k + comp] for comp in range(4)]
                across = [sums_s[4 * k + comp] for comp in range(4)]
                for u in range(GANG):
                    delta = [cols[u][axis] - rows[axis] for axis in range(3)]
                    dist2 = (
                        delta[0] * delta[0] + delta[1] * delta[1]
                        + (delta[2] * delta[2] + SOFTENING)
                    )
                    inverse = lax.rsqrt(dist2)
                    pot = cols[u][3] * rows[3] * inverse
                    cube = pot * (inverse * inverse)
                    parts = [pot] + [cube * delta[axis] for axis in range(3)]
                    sums[u] = [old + part for old, part in zip(sums[u], parts)]
                    across = [old + part for old, part in zip(across, parts)]
                for comp in range(4):
                    sums_s[4 * k + comp] = across[comp]
            for u in range(GANG):
                for comp in range(4):
                    at = pl.ds(pl.multiple_of(places[u] * 32 + 8 * comp, 8), 8)
                    acc_c[at, :] = acc_c[at, :] + sums[u][comp]
            return carry

        lax.fori_loop(0, meta[3, t], step, 0)
        for k in range(2 * level):
            res = acc_t[chunk, 8 * k : 8 * k + 8, :]
            for comp in range(4):
                whole = jnp.sum(sums_s[4 * k + comp], 1, keepdims=True)
                res = jnp.where(masks[comp], whole, res)
            acc_t[chunk, 8 * k : 8 * k + 8, :] = res

    def per_target(t, carry):
        level = lax.shift_right_logical(counts[t] - 1, 4)
        for want in range(NBUCKET):
            pl.when(level == want)(lambda want=want: run(want + 1, t))
        return carry

    lax.fori_loop(0, NBLK, per_target, 0)

    comp_of = lax.bitwise_and(lax.broadcasted_iota(I32, (8, LANES), 0), 3)
    sign = jnp.where(comp_of == 0, -1.0, 1.0)

    def fold(at):
        return jnp.concatenate(
            [jnp.sum(acc_c[pl.ds(at + 8 * r, 8), :], 0, keepdims=True) for r in range(8)], 0
        )

    for c in range(CHUNKS):
        back = acc_t[c].T
        for g in range(16):
            both = back[8 * g : 8 * g + 8, :] * sign - fold(c * 1024 + 64 * g)
            near_local[c * 128 + 8 * g : c * 128 + 8 * g + 8, :] = both

    def finish(g, carry):
        at = pl.multiple_of(g * 64, 64)
        near_inbound[pl.ds(pl.multiple_of(g * 8, 8), 8), :] = -fold(NBLK * 32 + at)
        return carry

    lax.fori_loop(0, INBOUND // 2, finish, 0, unroll=4)


def far_kernel(far_nodes, far_offset, moments, ops, offsets, far, binned):
    which = lax.broadcasted_iota(I32, (NOFF, LANES), 0)

    def gather(b, carry):
        total = jnp.zeros((NOFF, LANES), F32)
        for j in range(NFAR):
            row = jnp.broadcast_to(moments[pl.ds(far_nodes[j, b], 1), :], (NOFF, LANES))
            total = total + jnp.where(which == far_offset[j, b], row, 0.0)
        binned[pl.ds(pl.multiple_of(b * NOFF, NOFF), NOFF), :] = total
        return carry

    lax.fori_loop(0, NBLK, gather, 0)
    series = jnp.zeros((NBLK, NCOEF), F32)
    for o in range(NOFF):
        series = series + lax.dot_general(
            binned[pl.ds(o, NBLK, stride=NOFF), :][:, :NCOEF],
            ops[pl.ds(o, NCOEF, stride=NOFF), :],
            (((1,), (1,)), ((), ())),
            precision=lax.Precision.HIGHEST,
            preferred_element_type=F32,
        )
    binned[pl.ds(0, NBLK), pl.ds(0, NCOEF)] = series

    def group(g, carry):
        rows = pl.ds(pl.multiple_of(g * 8, 8), 8)
        x, y, z = (offsets[axis, rows, :] for axis in range(3))
        coefs = binned[rows, :]
        terms = monomial_chain(None, x, y, z)
        terms[0] = jnp.ones((8, LANES), F32)
        total = [jnp.zeros((8, LANES), F32) for comp in range(4)]
        for k, triple in enumerate(TRIPLES):
            coef = jnp.broadcast_to(coefs[:, k : k + 1], (8, LANES))
            total[0] = total[0] + (coef if k == 0 else coef * terms[k])
            for axis in range(3):
                power = triple[axis]
                if power > 0:
                    lower = list(triple)
                    lower[axis] -= 1
                    place = PLACE[tuple(lower)]
                    slope = coef if power == 1 else coef * float(power)
                    if place > 0:
                        slope = slope * terms[place]
                    total[axis + 1] = total[axis + 1] - slope
        for comp in range(4):
            far[comp, rows, :] = total[comp]
        return carry

    lax.fori_loop(0, NBLK // 8, group, 0)


def join_kernel(block_s, slots, near, returned, far, local, mass, field, total):
    total[...] = near[...]

    def back(r, carry):
        at = pl.ds(4 * block_s[r], 4)
        total[at, :] = total[at, :] + returned[pl.ds(4 * slots[r], 4), :]
        return carry

    lax.fori_loop(0, NROWS, back, 0, unroll=8)

    def group(g, carry):
        rows = pl.ds(pl.multiple_of(g * 8, 8), 8)
        live = local[pl.ds(32 * g + 3, 8, stride=4), :] > 0.0
        over = 1.0 / mass[rows, :]
        for comp in range(4):
            force = total[pl.ds(32 * g + comp, 8, stride=4), :]
            field[comp, rows, :] = jnp.where(live, far[comp, rows, :] + force * over, 0.0)
        return carry

    lax.fori_loop(0, NBLK // 8, group, 0)


def vmem():
    return pl.BlockSpec(memory_space=pltpu.VMEM)


def smem():
    return pl.BlockSpec(memory_space=pltpu.SMEM)


def params():
    return pltpu.CompilerParams(vmem_limit_bytes=VMEM_LIMIT)


def near_scratch():
    return [
        pltpu.VMEM((POOL_ROWS, LANES), F32),
        pltpu.VMEM((CHUNKS, 128, LANES), F32),
        pltpu.VMEM((CHUNKS, 128, LANES), F32),
        pltpu.VMEM(((POOL + 4) * 32, LANES), F32),
        pltpu.VMEM((64, 8, LANES), F32),
        pltpu.VMEM((64, 8, LANES), F32),
        pltpu.SMEM((ORDER + 8,), I32),
    ]


def shaped(*dims, dtype=F32):
    return jax.ShapeDtypeStruct(dims, dtype)


def body(
    positions, masses, counts, export_block, export_dest, near_pairs,
    node_of_block, far_nodes, far_offset, node_centers, m2l_ops,
):
    counts_row = counts.reshape(1, NBLK)
    local, outgoing, partial, slots, offsets = pl.pallas_call(
        prep_kernel,
        out_shape=(
            shaped(4 * NBLK, LANES), shaped(4 * INBOUND, LANES), shaped(NNODE, LANES),
            shaped(NROWS, dtype=I32), shaped(3, NBLK, LANES),
        ),
        in_specs=[smem()] * 3 + [vmem()] * 5,
        out_specs=(vmem(), vmem(), vmem(), smem(), vmem()),
        scratch_shapes=[pltpu.VMEM((NBLK, LANES), F32), pltpu.SMEM((NDEV,), I32)],
        compiler_params=params(),
        name="prep",
    )(
        export_block, export_dest.reshape(NROWS), node_of_block, positions, masses, counts_row,
        node_of_block.reshape(1, NBLK), node_centers,
    )
    shares = lax.all_to_all(
        partial.reshape(NDEV, NNODE // NDEV, LANES), AXES, split_axis=0, concat_axis=0, tiled=True
    )
    inbound = lax.all_to_all(
        outgoing.reshape(NDEV, 4 * SLOTS, LANES), AXES, split_axis=0, concat_axis=0, tiled=True
    ).reshape(4 * INBOUND, LANES)
    mine = jnp.sum(shares, 0)
    moments = lax.all_to_all(
        jnp.broadcast_to(mine[None], (NDEV, NNODE // NDEV, LANES)),
        AXES, split_axis=0, concat_axis=0, tiled=True,
    ).reshape(NNODE, LANES)
    meta = pl.pallas_call(
        build_kernel,
        out_shape=shaped(8, NPAIRS, dtype=I32),
        in_specs=[vmem()] * 3,
        out_specs=vmem(),
        compiler_params=params(),
        name="build",
    )(inbound, counts_row, jnp.transpose(near_pairs))
    near_local, near_inbound = pl.pallas_call(
        near_kernel,
        out_shape=(shaped(4 * NBLK, LANES), shaped(4 * INBOUND, LANES)),
        in_specs=[smem(), smem(), vmem(), vmem()],
        out_specs=(vmem(), vmem()),
        scratch_shapes=near_scratch(),
        compiler_params=params(),
        name="near",
    )(meta, counts, local, inbound)
    returned = lax.all_to_all(
        near_inbound.reshape(NDEV, 4 * SLOTS, LANES), AXES, split_axis=0, concat_axis=0, tiled=True
    ).reshape(4 * INBOUND, LANES)
    far = pl.pallas_call(
        far_kernel,
        out_shape=shaped(4, NBLK, LANES),
        in_specs=[smem(), smem(), vmem(), vmem(), vmem()],
        out_specs=vmem(),
        scratch_shapes=[pltpu.VMEM((NBLK * NOFF, LANES), F32)],
        compiler_params=params(),
        name="far",
    )(
        jnp.transpose(far_nodes), jnp.transpose(far_offset), moments,
        jnp.transpose(m2l_ops, (1, 0, 2)).reshape(NCOEF * NOFF, NCOEF), offsets,
    )
    return pl.pallas_call(
        join_kernel,
        out_shape=shaped(4, NBLK, LANES),
        in_specs=[smem(), smem()] + [vmem()] * 5,
        out_specs=vmem(),
        scratch_shapes=[pltpu.VMEM((4 * NBLK, LANES), F32)],
        compiler_params=params(),
        name="join",
    )(export_block, slots, near_local, returned, far, local, masses)


def solution(mesh):
    both = ("dom", "sub")
    placed = (
        P(None, both, None), P(both, None), P(both), P(both), P(both, None), P(both, None),
        P(both), P(both, None), P(both, None), P(), P(),
    )
    return jax.shard_map(
        body, mesh=mesh, in_specs=placed, out_specs=P(None, both, None), check_vma=False
    )
```

```python
import jax
import jax.numpy as jnp
import numpy as np
from jax import lax
from jax.experimental import pallas as pl
from jax.experimental.pallas import tpu as pltpu
from jax.sharding import PartitionSpec as P

SOFTENING = 0.0025
LANES = 128
NBLK = 128
NDEV = 128
SLOTS = 4
NNODE = 2048
NROWS = 256
NPAIRS = 1024
NFAR = 32
NOFF = 16
NCOEF = 84
INBOUND = NDEV * SLOTS
POOL = NBLK + INBOUND
NBUCKET = 8
AXES = ("dom", "sub")
VMEM_LIMIT = 58 * 1024 * 1024
F32 = jnp.float32
I32 = jnp.int32


def exponent_table():
    triples = []
    for degree in range(7):
        for first in range(degree, -1, -1):
            for second in range(degree - first, -1, -1):
                triples.append((first, second, degree - first - second))
    return triples


TRIPLES = exponent_table()
PLACE = {triple: place for place, triple in enumerate(TRIPLES)}


def monomial_chain(root, x, y, z):
    terms = []
    for a, b, c in TRIPLES:
        if a > 0:
            lower, axis = (a - 1, b, c), x
        elif b > 0:
            lower, axis = (a, b - 1, c), y
        elif c > 0:
            lower, axis = (a, b, c - 1), z
        else:
            terms.append(root)
            continue
        parent = terms[PLACE[lower]]
        terms.append(axis if parent is None else parent * axis)
    return terms


def export_kernel(block_s, dest_s, pos, mass, counts, local, outgoing, slots, used):
    lane = lax.broadcasted_iota(I32, (8, LANES), 1)
    sub = lax.broadcasted_iota(I32, (8, LANES), 0)
    counts_row = counts[...].astype(F32)
    for g in range(NBLK // 8):
        rows = slice(8 * g, 8 * g + 8)
        count_col = jnp.sum(jnp.where(lane == sub + 8 * g, counts_row, 0.0), 1, keepdims=True)
        weight = jnp.where(lane.astype(F32) < count_col, mass[rows, :], 0.0)
        for axis in range(3):
            local[pl.ds(32 * g + axis, 8, stride=4), :] = pos[axis, rows, :]
        local[pl.ds(32 * g + 3, 8, stride=4), :] = weight
    outgoing[...] = jnp.zeros_like(outgoing)

    def clear(i, carry):
        used[i] = 0
        return carry

    lax.fori_loop(0, NDEV, clear, 0, unroll=8)

    def place(r, carry):
        d = dest_s[r]
        k = used[d]
        used[d] = k + 1
        s = d * SLOTS + k
        slots[r] = s
        outgoing[pl.ds(4 * s, 4), :] = local[pl.ds(4 * block_s[r], 4), :]
        return carry

    lax.fori_loop(0, NROWS, place, 0, unroll=8)


def moment_kernel(node_s, pos, local, nodes, centers, partial, offsets, mom):
    lane = lax.broadcasted_iota(I32, (8, LANES), 1)
    sub = lax.broadcasted_iota(I32, (8, LANES), 0)
    wide = lax.broadcasted_iota(I32, (8, NNODE), 1).astype(F32)
    nodes_row = nodes[...].astype(F32)

    def group(g, carry):
        rows = pl.ds(pl.multiple_of(g * 8, 8), 8)
        diag = lane == sub + 8 * g
        node_col = jnp.sum(jnp.where(diag, nodes_row, 0.0), 1, keepdims=True)
        weight = local[pl.ds(32 * g + 3, 8, stride=4), :]
        picked = wide == node_col
        rel = []
        for axis in range(3):
            center = jnp.sum(
                jnp.where(picked, centers[axis : axis + 1, :], 0.0), 1, keepdims=True
            )
            rel.append(pos[axis, rows, :] - center)
            offsets[axis, rows, :] = rel[axis]
        terms = monomial_chain(weight, *rel)
        total = jnp.zeros((8, LANES), F32)
        for k in range(NCOEF):
            total = jnp.where(lane == k, jnp.sum(terms[k], 1, keepdims=True), total)
        mom[rows, :] = total
        return carry

    lax.fori_loop(0, NBLK // 8, group, 0)
    partial[...] = jnp.zeros_like(partial)

    def bin_block(b, carry):
        n = node_s[b]
        partial[pl.ds(n, 1), :] = partial[pl.ds(n, 1), :] + mom[pl.ds(b, 1), :]
        return carry

    lax.fori_loop(0, NBLK, bin_block, 0, unroll=8)


CHUNKS = NBLK // 32
BATCH = 32
WIDE = 4
COLUMNS = NPAIRS + NBLK


def build_kernel(inbound, counts, pairs, meta):
    wide_sub = lax.broadcasted_iota(I32, (8, NPAIRS), 0)
    square_lane = lax.broadcasted_iota(I32, (LANES, LANES), 1)
    square_sub = lax.broadcasted_iota(I32, (LANES, LANES), 0)
    lane = lax.broadcasted_iota(I32, (8, LANES), 1)
    sub = lax.broadcasted_iota(I32, (8, LANES), 0)
    counts_row = counts[...].astype(F32)
    target = pairs[0:1, :]
    source = pairs[1:2, :]

    def received(g, total):
        weight = inbound[pl.ds(32 * g + 3, 8, stride=4), :]
        col = jnp.sum(jnp.where(weight > 0.0, 1.0, 0.0), 1, keepdims=True)
        return total + jnp.where(wide_sub + 8 * g + NBLK == source, col, 0.0)

    live = lax.fori_loop(0, INBOUND // 8, received, jnp.zeros((8, NPAIRS), F32), unroll=8)
    for g in range(NBLK // 8):
        col = jnp.sum(jnp.where(lane == sub + 8 * g, counts_row, 0.0), 1, keepdims=True)
        live = live + jnp.where(wide_sub + 8 * g == source, col, 0.0)
    live = jnp.sum(live, 0, keepdims=True)
    totals = jnp.zeros((LANES, LANES), F32)
    for c in range(NPAIRS // LANES):
        at = slice(c * LANES, (c + 1) * LANES)
        totals = totals + jnp.where(square_sub == target[:, at], live[:, at], 0.0)
    totals = jnp.sum(totals, 1, keepdims=True)
    columns = jnp.floor((totals + (LANES - 1)) * (1.0 / LANES))
    diag = square_lane == square_sub
    columns_row = jnp.sum(jnp.where(diag, columns, 0.0), 0, keepdims=True)
    starts = jnp.sum(jnp.where(square_lane < square_sub, columns_row, 0.0), 1, keepdims=True)
    starts_row = jnp.sum(jnp.where(diag, starts, 0.0), 0, keepdims=True)
    upper = (square_sub < square_lane).astype(F32)
    running = starts * LANES
    for c in range(NPAIRS // LANES):
        at = slice(c * LANES, (c + 1) * LANES)
        hit = (square_sub == target[:, at]).astype(F32)
        held = hit * live[:, at]
        ahead = jnp.dot(held, upper, preferred_element_type=F32) + running
        meta[0:1, at] = jnp.sum(hit * ahead, 0, keepdims=True).astype(I32)
        running = running + jnp.sum(held, 1, keepdims=True)
    meta[1:2, :] = source * 256 + live.astype(I32)
    meta[2:8, :] = jnp.zeros((6, NPAIRS), I32)
    meta[2:3, 0:LANES] = starts_row.astype(I32)
    meta[3:4, 0:LANES] = columns_row.astype(I32)


def pack_kernel(meta, local, inbound, strips, pool, strips_b):
    lane = lax.broadcasted_iota(I32, (8, LANES), 1)
    upper = lax.broadcasted_iota(I32, (8, LANES), 0) >= 4

    def double(b, offset, blocks):
        two = blocks[pl.ds(pl.multiple_of(8 * b, 8), 8), :]
        turn = pltpu.roll(two, 4, 0)
        at = pl.multiple_of(16 * b + offset, 16)
        pool[pl.ds(at, 8), :] = jnp.where(upper, turn, two)
        pool[pl.ds(at + 8, 8), :] = jnp.where(upper, two, turn)

    def double_local(b, carry):
        double(b, 0, local)
        return carry

    def double_inbound(b, carry):
        double(b, 8 * NBLK, inbound)
        return carry

    lax.fori_loop(0, NBLK // 2, double_local, 0, unroll=8)
    lax.fori_loop(0, INBOUND // 2, double_inbound, 0, unroll=8)

    def clear(c, carry):
        strips[pl.ds(pl.multiple_of(c * 64, 64), 64), :] = jnp.zeros((64, LANES), F32)
        strips_b[pl.ds(pl.multiple_of(c * 64, 64), 64), :] = jnp.zeros((64, LANES), F32)
        return carry

    lax.fori_loop(0, (COLUMNS + 8) // 8, clear, 0)

    def pack(i, carry):
        ready = []
        for u in range(BATCH):
            where = meta[0, i * BATCH + u]
            what = meta[1, i * BATCH + u]
            first = lax.bitwise_and(where, LANES - 1)
            column = lax.shift_right_logical(where, 7) + 1
            block = lax.shift_right_logical(what, 8)
            last = first + lax.bitwise_and(what, 255)
            tile = pltpu.roll(pool[pl.ds(pl.multiple_of(8 * block, 8), 8), :], first, 1)
            keep = jnp.logical_and(place >= first, place < last)
            ready.append((column, jnp.where(keep, tile, 0.0)))
        for u, (column, tile) in enumerate(ready):
            at = pl.ds(pl.multiple_of(8 * column, 8), 8)
            held = (strips, strips_b)[u % 2]
            held[at, :] = held[at, :] + tile
        return carry

    place = jnp.where(upper, lane + LANES, lane)
    lax.fori_loop(0, NPAIRS // BATCH, pack, 0)

    def merge(c, carry):
        at = pl.ds(pl.multiple_of(c * 64, 64), 64)
        strips[at, :] = strips[at, :] + strips_b[at, :]
        return carry

    lax.fori_loop(0, (COLUMNS + 8) // 8, merge, 0)


def near_kernel(
    meta, counts, local, strips, near_local, near_inbound,
    turned, acc_t, acc, acc_b, results, rows_s, sums_s,
):
    nothing = jnp.zeros((8, LANES), F32)
    lane = lax.broadcasted_iota(I32, (8, LANES), 1)
    sub = lax.broadcasted_iota(I32, (8, LANES), 0)
    upper = sub >= 4

    def clear(b, carry):
        at = pl.ds(pl.multiple_of(b * 128, 128), 128)
        acc[at, :] = jnp.zeros((128, LANES), F32)
        acc_b[at, :] = jnp.zeros((128, LANES), F32)
        return carry

    lax.fori_loop(0, 8 * POOL // 128, clear, 0)
    place = jnp.where(upper, lane + LANES, lane)

    for c in range(NBLK // 8):
        whole = local[32 * c : 32 * c + 32, :]
        high = whole.astype(jnp.bfloat16).astype(F32)
        rest = whole - high
        middle = rest.astype(jnp.bfloat16).astype(F32)
        stack = [high, middle, rest - middle, jnp.zeros((32, LANES), F32)]
        turned[c] = jnp.concatenate(stack, 0).T.astype(jnp.bfloat16)
    for c in range(CHUNKS):
        acc_t[c] = jnp.zeros((128, LANES), F32)
    part_row = lax.bitwise_and(lax.broadcasted_iota(I32, (LANES, 4 * LANES), 0), 31)
    part_comp = lax.shift_right_logical(lax.broadcasted_iota(I32, (LANES, 4 * LANES), 1), 7)

    def spread(i, carry):
        pick = (part_row == 4 * i + part_comp).astype(F32).astype(jnp.bfloat16)
        for c in range(NBLK // 8):
            wide = jnp.dot(turned[c], pick, preferred_element_type=F32)
            for k in range(16):
                for comp in range(4):
                    rows_s[8 * c + i, 4 * k + comp] = wide[
                        8 * k : 8 * k + 8, LANES * comp : LANES * comp + LANES
                    ]
        return carry

    lax.fori_loop(0, 8, spread, 0)

    def lanes_of(t):
        first = lax.bitwise_and(t, 31) * 4
        return lax.shift_right_logical(t, 5), [
            jnp.zeros((8, LANES), I32) + (first + comp) for comp in range(4)
        ]

    low = [lax.bitwise_and(sub, bit) == 0 for bit in (1, 2, 4)]

    def fold(tiles):
        for place, bit in ((2, 4), (1, 2), (0, 1)):
            tiles = [
                jnp.where(low[place], tiles[i], tiles[i + bit])
                + jnp.where(
                    low[place],
                    pltpu.roll(tiles[i], 8 - bit, 0),
                    pltpu.roll(tiles[i + bit], bit, 0),
                )
                for i in range(bit)
            ]
        return tiles[0]

    def run(level, t):
        base = meta[2, t]
        count = meta[3, t]
        chunk, picks = lanes_of(t)
        for j in range(8 * level):
            sums_s[j] = nothing

        def columns(at, gang):
            cols, sums = [], []
            for u in range(gang):
                here = pl.multiple_of(8 * (at + u), 8)
                cols.append(
                    [
                        jnp.broadcast_to(strips[pl.ds(here + (8 + comp), 1), :], (8, LANES))
                        + jnp.broadcast_to(strips[pl.ds(here + (4 + comp), 1), :], (8, LANES))
                        for comp in range(4)
                    ]
                )
                sums.append([nothing] * 4)
            for k in range(2 * level):
                rows = [rows_s[t, 4 * k + comp] for comp in range(4)]
                across = [sums_s[4 * k + comp] for comp in range(4)]
                for u in range(gang):
                    delta = [cols[u][axis] - rows[axis] for axis in range(3)]
                    dist2 = (
                        delta[0] * delta[0] + delta[1] * delta[1]
                        + (delta[2] * delta[2] + SOFTENING)
                    )
                    inverse = lax.rsqrt(dist2)
                    pot = cols[u][3] * rows[3] * inverse
                    cube = pot * (inverse * inverse)
                    parts = [pot] + [cube * delta[axis] for axis in range(3)]
                    sums[u] = [old + part for old, part in zip(sums[u], parts)]
                    across = [old + part for old, part in zip(across, parts)]
                for comp in range(4):
                    sums_s[4 * k + comp] = across[comp]
            if gang == 1:
                results[pl.ds(4 * at, 4), :] = fold(sums[0] * 2)[:4, :]
            for u in range(0, gang - 1, 2):
                results[pl.ds(4 * (at + u), 8), :] = fold(sums[u] + sums[u + 1])

        def step(i, carry):
            columns(base + WIDE * i, WIDE)
            return carry

        lax.fori_loop(0, lax.div(count, WIDE), step, 0)
        size = WIDE // 2
        while size > 0:
            done = base + lax.bitwise_and(count, -2 * size)
            pl.when(lax.bitwise_and(count, size) > 0)(
                lambda done=done, size=size: columns(done, size)
            )
            size //= 2
        for k in range(2 * level):
            res = acc_t[chunk, 8 * k : 8 * k + 8, :]
            for comp in range(4):
                whole = jnp.sum(sums_s[4 * k + comp], 1, keepdims=True)
                res = jnp.where(lane == picks[comp], whole, res)
            acc_t[chunk, 8 * k : 8 * k + 8, :] = res

    def per_target(t, carry):
        level = lax.shift_right_logical(counts[t] - 1, 4)

        def choose(least, most):
            if least == most:
                run(least + 1, t)
                return
            middle = (least + most + 1) // 2
            pl.when(level < middle)(lambda: choose(least, middle - 1))
            pl.when(level >= middle)(lambda: choose(middle, most))

        choose(0, NBUCKET - 1)
        return carry

    lax.fori_loop(0, NBLK, per_target, 0)

    def unpack(i, carry):
        ready = []
        for u in range(BATCH):
            where = meta[0, i * BATCH + u]
            what = meta[1, i * BATCH + u]
            first = lax.bitwise_and(where, LANES - 1)
            column = lax.shift_right_logical(where, 7)
            block = lax.shift_right_logical(what, 8)
            last = first + lax.bitwise_and(what, 255)
            tile = results[pl.ds(4 * column, 8), :]
            keep = jnp.logical_and(place >= first, place < last)
            tile = jnp.where(keep, tile, 0.0)
            ready.append((block, pltpu.roll(tile, lax.bitwise_and(LANES - first, LANES - 1), 1)))
        for u, (block, tile) in enumerate(ready):
            at = pl.ds(pl.multiple_of(8 * block, 8), 8)
            held = (acc, acc_b)[u % 2]
            held[at, :] = held[at, :] + tile
        return carry

    lax.fori_loop(0, NPAIRS // BATCH, unpack, 0)

    sign = jnp.where(lax.bitwise_and(sub, 3) == 0, -1.0, 1.0)

    def joined(at):
        one = acc[pl.ds(at, 8), :] + acc_b[pl.ds(at, 8), :]
        two = acc[pl.ds(at + 8, 8), :] + acc_b[pl.ds(at + 8, 8), :]
        one = one + pltpu.roll(one, 4, 0)
        two = two + pltpu.roll(two, 4, 0)
        return jnp.where(upper, two, one)

    for c in range(CHUNKS):
        back = acc_t[c].T
        for g in range(16):
            both = back[8 * g : 8 * g + 8, :] * sign - joined(c * 256 + 16 * g)
            near_local[c * 128 + 8 * g : c * 128 + 8 * g + 8, :] = both

    def finish(g, carry):
        at = pl.multiple_of(g * 16, 16)
        near_inbound[pl.ds(pl.multiple_of(g * 8, 8), 8), :] = -joined(NBLK * 8 + at)
        return carry

    lax.fori_loop(0, INBOUND // 2, finish, 0, unroll=8)


def far_kernel(far_nodes, far_offset, moments, ops, offsets, far, binned):
    which = lax.broadcasted_iota(I32, (NOFF, LANES), 0)

    def gather(b, carry):
        total = jnp.zeros((NOFF, LANES), F32)
        for j in range(NFAR):
            row = jnp.broadcast_to(moments[pl.ds(far_nodes[j, b], 1), :], (NOFF, LANES))
            total = total + jnp.where(which == far_offset[j, b], row, 0.0)
        binned[pl.ds(pl.multiple_of(b * NOFF, NOFF), NOFF), :] = total
        return carry

    lax.fori_loop(0, NBLK, gather, 0)
    series = jnp.zeros((NBLK, NCOEF), F32)
    for o in range(NOFF):
        series = series + lax.dot_general(
            binned[pl.ds(o, NBLK, stride=NOFF), :][:, :NCOEF],
            ops[pl.ds(o, NCOEF, stride=NOFF), :],
            (((1,), (1,)), ((), ())),
            precision=lax.Precision.HIGHEST,
            preferred_element_type=F32,
        )
    binned[pl.ds(0, NBLK), pl.ds(0, NCOEF)] = series

    def group(g, carry):
        rows = pl.ds(pl.multiple_of(g * 8, 8), 8)
        x, y, z = (offsets[axis, rows, :] for axis in range(3))
        coefs = binned[rows, :]
        terms = monomial_chain(None, x, y, z)
        terms[0] = jnp.ones((8, LANES), F32)
        total = [jnp.zeros((8, LANES), F32) for comp in range(4)]
        for k, triple in enumerate(TRIPLES):
            coef = jnp.broadcast_to(coefs[:, k : k + 1], (8, LANES))
            total[0] = total[0] + (coef if k == 0 else coef * terms[k])
            for axis in range(3):
                power = triple[axis]
                if power > 0:
                    lower = list(triple)
                    lower[axis] -= 1
                    place = PLACE[tuple(lower)]
                    slope = coef if power == 1 else coef * float(power)
                    if place > 0:
                        slope = slope * terms[place]
                    total[axis + 1] = total[axis + 1] - slope
        for comp in range(4):
            far[comp, rows, :] = total[comp]
        return carry

    lax.fori_loop(0, NBLK // 8, group, 0)


def join_kernel(block_s, slots, near, returned, far, local, mass, field, total, total_b):
    total[...] = near[...]
    total_b[...] = jnp.zeros_like(total_b)

    def back(i, carry):
        ready = [returned[pl.ds(4 * slots[8 * i + u], 4), :] for u in range(8)]
        for u in range(8):
            at = pl.ds(4 * block_s[8 * i + u], 4)
            held = (total, total_b)[u % 2]
            held[at, :] = held[at, :] + ready[u]
        return carry

    lax.fori_loop(0, NROWS // 8, back, 0)

    def group(g, carry):
        rows = pl.ds(pl.multiple_of(g * 8, 8), 8)
        live = local[pl.ds(32 * g + 3, 8, stride=4), :] > 0.0
        over = 1.0 / mass[rows, :]
        for comp in range(4):
            at = pl.ds(32 * g + comp, 8, stride=4)
            force = total[at, :] + total_b[at, :]
            field[comp, rows, :] = jnp.where(live, far[comp, rows, :] + force * over, 0.0)
        return carry

    lax.fori_loop(0, NBLK // 8, group, 0)


def vmem():
    return pl.BlockSpec(memory_space=pltpu.VMEM)


def smem():
    return pl.BlockSpec(memory_space=pltpu.SMEM)


def params():
    return pltpu.CompilerParams(vmem_limit_bytes=VMEM_LIMIT)


def near_scratch():
    return [
        pltpu.VMEM((NBLK // 8, 128, LANES), jnp.bfloat16),
        pltpu.VMEM((CHUNKS, 128, LANES), F32),
        pltpu.VMEM((8 * POOL, LANES), F32),
        pltpu.VMEM((8 * POOL, LANES), F32),
        pltpu.VMEM((4 * (COLUMNS + 8), LANES), F32),
        pltpu.VMEM((NBLK, 64, 8, LANES), F32),
        pltpu.VMEM((64, 8, LANES), F32),
    ]


def near_field(meta, counts, local, inbound):
    strips = pl.pallas_call(
        pack_kernel,
        out_shape=shaped(8 * (COLUMNS + 8), LANES),
        in_specs=[smem(), vmem(), vmem()],
        out_specs=vmem(),
        scratch_shapes=[
            pltpu.VMEM((8 * POOL, LANES), F32), pltpu.VMEM((8 * (COLUMNS + 8), LANES), F32),
        ],
        compiler_params=params(),
        cost_estimate=costs(10),
        name="pack",
    )(meta, local, inbound)
    return pl.pallas_call(
        near_kernel,
        out_shape=(shaped(4 * NBLK, LANES), shaped(4 * INBOUND, LANES)),
        in_specs=[smem(), smem(), vmem(), vmem()],
        out_specs=(vmem(), vmem()),
        scratch_shapes=near_scratch(),
        compiler_params=params(),
        cost_estimate=costs(60),
        name="near",
    )(meta, counts, local, strips)


def costs(microseconds):
    return pl.CostEstimate(
        flops=int(microseconds * 1.15e9), bytes_accessed=1 << 20, transcendentals=0
    )


def shaped(*dims, dtype=F32):
    return jax.ShapeDtypeStruct(dims, dtype)


def body(
    positions, masses, counts, export_block, export_dest, near_pairs,
    node_of_block, far_nodes, far_offset, node_centers, m2l_ops,
):
    counts_row = counts.reshape(1, NBLK)
    local, outgoing, slots = pl.pallas_call(
        export_kernel,
        out_shape=(
            shaped(4 * NBLK, LANES), shaped(4 * INBOUND, LANES), shaped(NROWS, dtype=I32),
        ),
        in_specs=[smem()] * 2 + [vmem()] * 3,
        out_specs=(vmem(), vmem(), smem()),
        scratch_shapes=[pltpu.SMEM((NDEV,), I32)],
        compiler_params=params(),
        cost_estimate=costs(4),
        name="export",
    )(export_block, export_dest.reshape(NROWS), positions, masses, counts_row)
    inbound = lax.all_to_all(
        outgoing.reshape(NDEV, 4 * SLOTS, LANES), AXES, split_axis=0, concat_axis=0, tiled=True
    ).reshape(4 * INBOUND, LANES)
    partial, offsets = pl.pallas_call(
        moment_kernel,
        out_shape=(shaped(NNODE, LANES), shaped(3, NBLK, LANES)),
        in_specs=[smem()] + [vmem()] * 4,
        out_specs=(vmem(), vmem()),
        scratch_shapes=[pltpu.VMEM((NBLK, LANES), F32)],
        compiler_params=params(),
        cost_estimate=costs(8),
        name="moment",
    )(node_of_block, positions, local, node_of_block.reshape(1, NBLK), node_centers)
    partial, inbound = lax.optimization_barrier((partial, inbound))
    shares = lax.all_to_all(
        partial.reshape(NDEV, NNODE // NDEV, LANES), AXES, split_axis=0, concat_axis=0, tiled=True
    )
    mine = jnp.sum(shares, 0)
    moments = lax.all_to_all(
        jnp.broadcast_to(mine[None], (NDEV, NNODE // NDEV, LANES)),
        AXES, split_axis=0, concat_axis=0, tiled=True,
    ).reshape(NNODE, LANES)
    meta = pl.pallas_call(
        build_kernel,
        out_shape=shaped(8, NPAIRS, dtype=I32),
        in_specs=[vmem()] * 3,
        out_specs=vmem(),
        compiler_params=params(),
        cost_estimate=costs(4),
        name="build",
    )(inbound, counts_row, jnp.transpose(near_pairs))
    near_local, near_inbound = near_field(meta, counts, local, inbound)
    returned = lax.all_to_all(
        near_inbound.reshape(NDEV, 4 * SLOTS, LANES), AXES, split_axis=0, concat_axis=0, tiled=True
    ).reshape(4 * INBOUND, LANES)
    far = pl.pallas_call(
        far_kernel,
        out_shape=shaped(4, NBLK, LANES),
        in_specs=[smem(), smem(), vmem(), vmem(), vmem()],
        out_specs=vmem(),
        scratch_shapes=[pltpu.VMEM((NBLK * NOFF, LANES), F32)],
        compiler_params=params(),
        cost_estimate=costs(13),
        name="far",
    )(
        jnp.transpose(far_nodes), jnp.transpose(far_offset), moments,
        jnp.transpose(m2l_ops, (1, 0, 2)).reshape(NCOEF * NOFF, NCOEF), offsets,
    )
    return pl.pallas_call(
        join_kernel,
        out_shape=shaped(4, NBLK, LANES),
        in_specs=[smem(), smem()] + [vmem()] * 5,
        out_specs=vmem(),
        scratch_shapes=[pltpu.VMEM((4 * NBLK, LANES), F32)] * 2,
        compiler_params=params(),
        cost_estimate=costs(4),
        name="join",
    )(export_block, slots, near_local, returned, far, local, masses)


def solution(mesh):
    both = ("dom", "sub")
    placed = (
        P(None, both, None), P(both, None), P(both), P(both), P(both, None), P(both, None),
        P(both), P(both, None), P(both, None), P(), P(),
    )
    return jax.shard_map(
        body, mesh=mesh, in_specs=placed, out_specs=P(None, both, None), check_vma=False
    )
```

```python
import jax
import jax.numpy as jnp
import numpy as np
from jax import lax
from jax.experimental import pallas as pl
from jax.experimental.pallas import tpu as pltpu
from jax.sharding import PartitionSpec as P

SOFTENING = 0.0025
LANES = 128
NBLK = 128
NDEV = 128
SLOTS = 4
NNODE = 2048
HALF = NNODE // 2
NROWS = 256
NPAIRS = 1024
NFAR = 32
NOFF = 16
NCOEF = 84
INBOUND = NDEV * SLOTS
POOL = NBLK + INBOUND
NBUCKET = 16
AXES = ("dom", "sub")
F32 = jnp.float32
I32 = jnp.int32


def exponent_table():
    triples = []
    for degree in range(7):
        for first in range(degree, -1, -1):
            for second in range(degree - first, -1, -1):
                triples.append((first, second, degree - first - second))
    return triples


TRIPLES = exponent_table()
PLACE = {triple: place for place, triple in enumerate(TRIPLES)}


def monomial_chain(root, x, y, z):
    terms = []
    for a, b, c in TRIPLES:
        if a > 0:
            lower, axis = (a - 1, b, c), x
        elif b > 0:
            lower, axis = (a, b - 1, c), y
        elif c > 0:
            lower, axis = (a, b, c - 1), z
        else:
            terms.append(root)
            continue
        parent = terms[PLACE[lower]]
        terms.append(axis if parent is None else parent * axis)
    return terms


def own_flip():
    return lax.bitwise_and(lax.axis_index("dom"), 1) * HALF


def export_kernel(block_s, dest_s, pos, mass, counts, local, outgoing, slots, used):
    lane = lax.broadcasted_iota(I32, (8, LANES), 1)
    sub = lax.broadcasted_iota(I32, (8, LANES), 0)
    counts_row = counts[...].astype(F32)
    for g in range(NBLK // 8):
        rows = slice(8 * g, 8 * g + 8)
        count_col = jnp.sum(jnp.where(lane == sub + 8 * g, counts_row, 0.0), 1, keepdims=True)
        weight = jnp.where(lane.astype(F32) < count_col, mass[rows, :], 0.0)
        for axis in range(3):
            local[pl.ds(32 * g + axis, 8, stride=4), :] = pos[axis, rows, :]
        local[pl.ds(32 * g + 3, 8, stride=4), :] = weight
    outgoing[...] = jnp.zeros_like(outgoing)

    def clear(i, carry):
        used[i] = 0
        return carry

    lax.fori_loop(0, NDEV, clear, 0, unroll=8)

    def place(r, carry):
        d = dest_s[r]
        k = used[d]
        used[d] = k + 1
        s = d * SLOTS + k
        slots[r] = s
        outgoing[pl.ds(4 * s, 4), :] = local[pl.ds(4 * block_s[r], 4), :]
        return carry

    lax.fori_loop(0, NROWS, place, 0, unroll=8)


def moment_kernel(
    node_s, pos, local, nodes, centers, own_half, other_half, offsets, turned, mom, partial
):
    for c in range(NBLK // 8):
        whole = local[32 * c : 32 * c + 32, :]
        high = whole.astype(jnp.bfloat16).astype(F32)
        rest = whole - high
        middle = rest.astype(jnp.bfloat16).astype(F32)
        stack = [high, middle, rest - middle, jnp.zeros((32, LANES), F32)]
        turned[c] = jnp.concatenate(stack, 0).T.astype(jnp.bfloat16)
    lane = lax.broadcasted_iota(I32, (8, LANES), 1)
    sub = lax.broadcasted_iota(I32, (8, LANES), 0)
    wide = lax.broadcasted_iota(I32, (8, NNODE), 1).astype(F32)
    nodes_row = nodes[...].astype(F32)

    def group(g, carry):
        rows = pl.ds(pl.multiple_of(g * 8, 8), 8)
        diag = lane == sub + 8 * g
        node_col = jnp.sum(jnp.where(diag, nodes_row, 0.0), 1, keepdims=True)
        weight = local[pl.ds(32 * g + 3, 8, stride=4), :]
        picked = wide == node_col
        rel = []
        for axis in range(3):
            center = jnp.sum(
                jnp.where(picked, centers[axis : axis + 1, :], 0.0), 1, keepdims=True
            )
            rel.append(pos[axis, rows, :] - center)
            offsets[axis, rows, :] = rel[axis]
        terms = monomial_chain(weight, *rel)
        total = jnp.zeros((8, LANES), F32)
        for k in range(NCOEF):
            total = jnp.where(lane == k, jnp.sum(terms[k], 1, keepdims=True), total)
        mom[rows, :] = total
        return carry

    lax.fori_loop(0, NBLK // 8, group, 0)
    partial[...] = jnp.zeros_like(partial)

    def bin_block(b, carry):
        n = lax.bitwise_xor(node_s[b], flip)
        partial[pl.ds(n, 1), :] = partial[pl.ds(n, 1), :] + mom[pl.ds(b, 1), :]
        return carry

    flip = own_flip()
    lax.fori_loop(0, NBLK, bin_block, 0, unroll=8)
    own_half[...] = partial[pl.ds(0, HALF), :]
    other_half[...] = partial[pl.ds(HALF, HALF), :]


CHUNKS = NBLK // 32
BATCH = 32
WIDE = 4
COLUMNS = NPAIRS + NBLK


def build_kernel(inbound, counts, pairs, meta):
    wide_sub = lax.broadcasted_iota(I32, (8, NPAIRS), 0)
    square_lane = lax.broadcasted_iota(I32, (LANES, LANES), 1)
    square_sub = lax.broadcasted_iota(I32, (LANES, LANES), 0)
    lane = lax.broadcasted_iota(I32, (8, LANES), 1)
    sub = lax.broadcasted_iota(I32, (8, LANES), 0)
    counts_row = counts[...].astype(F32)
    target = pairs[0:1, :]
    source = pairs[1:2, :]

    def received(g, total):
        weight = inbound[pl.ds(32 * g + 3, 8, stride=4), :]
        col = jnp.sum(jnp.where(weight > 0.0, 1.0, 0.0), 1, keepdims=True)
        return total + jnp.where(wide_sub + 8 * g + NBLK == source, col, 0.0)

    live = lax.fori_loop(0, INBOUND // 8, received, jnp.zeros((8, NPAIRS), F32), unroll=8)
    for g in range(NBLK // 8):
        col = jnp.sum(jnp.where(lane == sub + 8 * g, counts_row, 0.0), 1, keepdims=True)
        live = live + jnp.where(wide_sub + 8 * g == source, col, 0.0)
    live = jnp.sum(live, 0, keepdims=True)
    totals = jnp.zeros((LANES, LANES), F32)
    for c in range(NPAIRS // LANES):
        at = slice(c * LANES, (c + 1) * LANES)
        totals = totals + jnp.where(square_sub == target[:, at], live[:, at], 0.0)
    totals = jnp.sum(totals, 1, keepdims=True)
    columns = jnp.floor((totals + (LANES - 1)) * (1.0 / LANES))
    diag = square_lane == square_sub
    columns_row = jnp.sum(jnp.where(diag, columns, 0.0), 0, keepdims=True)
    starts = jnp.sum(jnp.where(square_lane < square_sub, columns_row, 0.0), 1, keepdims=True)
    starts_row = jnp.sum(jnp.where(diag, starts, 0.0), 0, keepdims=True)
    upper = (square_sub < square_lane).astype(F32)
    running = starts * LANES
    for c in range(NPAIRS // LANES):
        at = slice(c * LANES, (c + 1) * LANES)
        hit = (square_sub == target[:, at]).astype(F32)
        held = hit * live[:, at]
        ahead = jnp.dot(held, upper, preferred_element_type=F32) + running
        meta[0:1, at] = jnp.sum(hit * ahead, 0, keepdims=True).astype(I32)
        running = running + jnp.sum(held, 1, keepdims=True)
    meta[1:2, :] = source * 256 + live.astype(I32)
    meta[2:8, :] = jnp.zeros((6, NPAIRS), I32)
    meta[2:3, 0:LANES] = starts_row.astype(I32)
    meta[3:4, 0:LANES] = columns_row.astype(I32)


def pack_kernel(meta, local, inbound, packed, pool, strips, strips_b):
    lane = lax.broadcasted_iota(I32, (8, LANES), 1)
    upper = lax.broadcasted_iota(I32, (8, LANES), 0) >= 4

    def double(b, offset, blocks):
        two = blocks[pl.ds(pl.multiple_of(8 * b, 8), 8), :]
        turn = pltpu.roll(two, 4, 0)
        at = pl.multiple_of(16 * b + offset, 16)
        pool[pl.ds(at, 8), :] = jnp.where(upper, turn, two)
        pool[pl.ds(at + 8, 8), :] = jnp.where(upper, two, turn)

    def double_local(b, carry):
        double(b, 0, local)
        return carry

    def double_inbound(b, carry):
        double(b, 8 * NBLK, inbound)
        return carry

    lax.fori_loop(0, NBLK // 2, double_local, 0, unroll=8)
    lax.fori_loop(0, INBOUND // 2, double_inbound, 0, unroll=8)

    def clear(c, carry):
        strips[pl.ds(pl.multiple_of(c * 64, 64), 64), :] = jnp.zeros((64, LANES), F32)
        strips_b[pl.ds(pl.multiple_of(c * 64, 64), 64), :] = jnp.zeros((64, LANES), F32)
        return carry

    lax.fori_loop(0, (COLUMNS + 8) // 8, clear, 0)

    def pack(i, carry):
        ready = []
        for u in range(BATCH):
            where = meta[0, i * BATCH + u]
            what = meta[1, i * BATCH + u]
            first = lax.bitwise_and(where, LANES - 1)
            column = lax.shift_right_logical(where, 7) + 1
            block = lax.shift_right_logical(what, 8)
            last = first + lax.bitwise_and(what, 255)
            tile = pltpu.roll(pool[pl.ds(pl.multiple_of(8 * block, 8), 8), :], first, 1)
            keep = jnp.logical_and(place >= first, place < last)
            ready.append((column, jnp.where(keep, tile, 0.0)))
        for u, (column, tile) in enumerate(ready):
            at = pl.ds(pl.multiple_of(8 * column, 8), 8)
            held = (strips, strips_b)[u % 2]
            held[at, :] = held[at, :] + tile
        return carry

    place = jnp.where(upper, lane + LANES, lane)
    lax.fori_loop(0, NPAIRS // BATCH, pack, 0)

    def merge(g, carry):
        at = pl.multiple_of(32 * g, 32)
        before = strips[pl.ds(at, 8), :] + strips_b[pl.ds(at, 8), :]
        before = pltpu.roll(before, 4, 0)
        for u in (1, 3):
            one = strips[pl.ds(at + 8 * u, 8), :] + strips_b[pl.ds(at + 8 * u, 8), :]
            two = strips[pl.ds(at + 8 * u + 8, 8), :] + strips_b[pl.ds(at + 8 * u + 8, 8), :]
            after = pltpu.roll(two, 4, 0)
            packed[pl.ds(pl.multiple_of(16 * g + 4 * u - 4, 8), 8), :] = jnp.where(
                upper, after, one
            ) + jnp.where(upper, one, before)
            before = after
        return carry

    lax.fori_loop(0, COLUMNS // 4, merge, 0, unroll=4)


def near_kernel(
    meta, counts, turned, strips, near_local, near_inbound,
    acc_t, acc, acc_b, results, rows_s, sums_s,
):
    nothing = jnp.zeros((8, LANES), F32)
    lane = lax.broadcasted_iota(I32, (8, LANES), 1)
    sub = lax.broadcasted_iota(I32, (8, LANES), 0)
    upper = sub >= 4

    def clear(b, carry):
        at = pl.ds(pl.multiple_of(b * 128, 128), 128)
        for held in (acc, acc_b):
            held[at, :] = jnp.zeros((128, LANES), F32)
        return carry

    lax.fori_loop(0, 8 * POOL // 128, clear, 0)
    place = jnp.where(upper, lane + LANES, lane)

    for c in range(CHUNKS):
        acc_t[c] = jnp.zeros((128, LANES), F32)
    part_row = lax.bitwise_and(lax.broadcasted_iota(I32, (LANES, 4 * LANES), 0), 31)
    part_comp = lax.shift_right_logical(lax.broadcasted_iota(I32, (LANES, 4 * LANES), 1), 7)

    def spread(i, carry):
        pick = (part_row == 4 * i + part_comp).astype(F32).astype(jnp.bfloat16)
        for c in range(NBLK // 8):
            wide = jnp.dot(turned[c], pick, preferred_element_type=F32)
            for k in range(16):
                for comp in range(4):
                    rows_s[8 * c + i, 4 * k + comp] = wide[
                        8 * k : 8 * k + 8, LANES * comp : LANES * comp + LANES
                    ]
        return carry

    lax.fori_loop(0, 8, spread, 0)

    def lanes_of(t):
        first = lax.bitwise_and(t, 31) * 4
        return lax.shift_right_logical(t, 5), [
            jnp.zeros((8, LANES), I32) + (first + comp) for comp in range(4)
        ]

    low = [lax.bitwise_and(sub, bit) == 0 for bit in (1, 2, 4)]

    def fold(tiles):
        for place, bit in ((2, 4), (1, 2), (0, 1)):
            tiles = [
                jnp.where(low[place], tiles[i], tiles[i + bit])
                + jnp.where(
                    low[place],
                    pltpu.roll(tiles[i], 8 - bit, 0),
                    pltpu.roll(tiles[i + bit], bit, 0),
                )
                for i in range(bit)
            ]
        return tiles[0]

    def run(level, t):
        base = meta[2, t]
        count = meta[3, t]
        chunk, picks = lanes_of(t)
        for j in range(4 * level):
            sums_s[j] = nothing

        def columns(at, gang):
            cols, sums = [], []
            for u in range(gang):
                cols.append(
                    [
                        jnp.broadcast_to(strips[pl.ds(4 * (at + u) + comp, 1), :], (8, LANES))
                        for comp in range(4)
                    ]
                )
                sums.append([nothing] * 4)
            for k in range(level):
                rows = [rows_s[t, 4 * k + comp] for comp in range(4)]
                across = [sums_s[4 * k + comp] for comp in range(4)]
                for u in range(gang):
                    delta = [cols[u][axis] - rows[axis] for axis in range(3)]
                    dist2 = (
                        delta[0] * delta[0] + delta[1] * delta[1]
                        + (delta[2] * delta[2] + SOFTENING)
                    )
                    inverse = lax.rsqrt(dist2)
                    pot = cols[u][3] * rows[3] * inverse
                    cube = pot * (inverse * inverse)
                    parts = [pot] + [cube * delta[axis] for axis in range(3)]
                    sums[u] = [old + part for old, part in zip(sums[u], parts)]
                    across = [old + part for old, part in zip(across, parts)]
                for comp in range(4):
                    sums_s[4 * k + comp] = across[comp]
            for u in range(0, gang, 2):
                both = fold(sums[u] + sums[min(u + 1, gang - 1)])
                swapped = pltpu.roll(both, 4, 0)
                here = pl.multiple_of(8 * (at + u) + 8, 8)
                results[pl.ds(here, 8), :] = both
                results[pl.ds(here - 4, 4), :] = swapped[4:8, :]
                if gang > 1:
                    results[pl.ds(here + 8, 4), :] = swapped[0:4, :]

        def step(i, carry):
            columns(base + WIDE * i, WIDE)
            return carry

        lax.fori_loop(0, lax.div(count, WIDE), step, 0)
        size = WIDE // 2
        while size > 0:
            done = base + lax.bitwise_and(count, -2 * size)
            pl.when(lax.bitwise_and(count, size) > 0)(
                lambda done=done, size=size: columns(done, size)
            )
            size //= 2
        for k in range(level):
            res = acc_t[chunk, 8 * k : 8 * k + 8, :]
            for comp in range(4):
                whole = jnp.sum(sums_s[4 * k + comp], 1, keepdims=True)
                res = jnp.where(lane == picks[comp], whole, res)
            acc_t[chunk, 8 * k : 8 * k + 8, :] = res

    def per_target(t, carry):
        level = lax.shift_right_logical(counts[t] - 1, 3)

        def choose(least, most):
            if least == most:
                run(least + 1, t)
                return
            middle = (least + most + 1) // 2
            pl.when(level < middle)(lambda: choose(least, middle - 1))
            pl.when(level >= middle)(lambda: choose(middle, most))

        choose(0, NBUCKET - 1)
        return carry

    lax.fori_loop(0, NBLK, per_target, 0)

    def unpack(i, carry):
        ready = []
        for u in range(BATCH):
            where = meta[0, i * BATCH + u]
            what = meta[1, i * BATCH + u]
            first = lax.bitwise_and(where, LANES - 1)
            column = lax.shift_right_logical(where, 7) + 1
            block = lax.shift_right_logical(what, 8)
            last = first + lax.bitwise_and(what, 255)
            tile = results[pl.ds(pl.multiple_of(8 * column, 8), 8), :]
            keep = jnp.logical_and(place >= first, place < last)
            tile = jnp.where(keep, tile, 0.0)
            ready.append((block, pltpu.roll(tile, lax.bitwise_and(LANES - first, LANES - 1), 1)))
        for u, (block, tile) in enumerate(ready):
            at = pl.ds(pl.multiple_of(8 * block, 8), 8)
            held = (acc, acc_b)[u % 2]
            held[at, :] = held[at, :] + tile
        return carry

    lax.fori_loop(0, NPAIRS // BATCH, unpack, 0)

    sign = jnp.where(lax.bitwise_and(sub, 3) == 0, -1.0, 1.0)

    def joined(at):
        one, two = (
            acc[pl.ds(here, 8), :] + acc_b[pl.ds(here, 8), :]
            for here in (at, at + 8)
        )
        one = one + pltpu.roll(one, 4, 0)
        two = two + pltpu.roll(two, 4, 0)
        return jnp.where(upper, two, one)

    for c in range(CHUNKS):
        back = acc_t[c].T
        for g in range(16):
            both = back[8 * g : 8 * g + 8, :] * sign - joined(c * 256 + 16 * g)
            near_local[c * 128 + 8 * g : c * 128 + 8 * g + 8, :] = both

    def finish(g, carry):
        at = pl.multiple_of(g * 16, 16)
        near_inbound[pl.ds(pl.multiple_of(g * 8, 8), 8), :] = -joined(NBLK * 8 + at)
        return carry

    lax.fori_loop(0, INBOUND // 2, finish, 0, unroll=8)


def far_kernel(
    far_nodes, far_offset, own_half, other_half, ops, offsets, far, binned, moments
):
    moments[pl.ds(0, HALF), :] = own_half[...]
    moments[pl.ds(HALF, HALF), :] = other_half[...]
    flip = own_flip()
    which = lax.broadcasted_iota(I32, (NOFF, LANES), 0)

    def gather(b, carry):
        total = jnp.zeros((NOFF, LANES), F32)
        for j in range(NFAR):
            node = lax.bitwise_xor(far_nodes[j, b], flip)
            row = jnp.broadcast_to(moments[pl.ds(node, 1), :], (NOFF, LANES))
            total = total + jnp.where(which == far_offset[j, b], row, 0.0)
        binned[pl.ds(pl.multiple_of(b * NOFF, NOFF), NOFF), :] = total
        return carry

    lax.fori_loop(0, NBLK, gather, 0, unroll=2)
    series = jnp.zeros((NBLK, NCOEF), F32)
    for o in range(NOFF):
        series = series + lax.dot_general(
            binned[pl.ds(o, NBLK, stride=NOFF), :][:, :NCOEF],
            ops[pl.ds(o, NCOEF, stride=NOFF), :],
            (((1,), (1,)), ((), ())),
            precision=lax.Precision.HIGHEST,
            preferred_element_type=F32,
        )
    binned[pl.ds(0, NBLK), pl.ds(0, NCOEF)] = series

    def group(g, carry):
        rows = pl.ds(pl.multiple_of(g * 8, 8), 8)
        x, y, z = (offsets[axis, rows, :] for axis in range(3))
        coefs = binned[rows, :]
        terms = monomial_chain(None, x, y, z)
        terms[0] = jnp.ones((8, LANES), F32)
        total = [jnp.zeros((8, LANES), F32) for comp in range(4)]
        for k, triple in enumerate(TRIPLES):
            coef = jnp.broadcast_to(coefs[:, k : k + 1], (8, LANES))
            total[0] = total[0] + (coef if k == 0 else coef * terms[k])
            for axis in range(3):
                power = triple[axis]
                if power > 0:
                    lower = list(triple)
                    lower[axis] -= 1
                    place = PLACE[tuple(lower)]
                    slope = coef if power == 1 else coef * float(power)
                    if place > 0:
                        slope = slope * terms[place]
                    total[axis + 1] = total[axis + 1] - slope
        for comp in range(4):
            far[comp, rows, :] = total[comp]
        return carry

    lax.fori_loop(0, NBLK // 8, group, 0)


def join_kernel(block_s, slots, near, returned, far, local, mass, field, total, total_b):
    total[...] = near[...]
    total_b[...] = jnp.zeros_like(total_b)

    def back(i, carry):
        ready = [returned[pl.ds(4 * slots[8 * i + u], 4), :] for u in range(8)]
        for u in range(8):
            at = pl.ds(4 * block_s[8 * i + u], 4)
            held = (total, total_b)[u % 2]
            held[at, :] = held[at, :] + ready[u]
        return carry

    lax.fori_loop(0, NROWS // 8, back, 0)

    def group(g, carry):
        rows = pl.ds(pl.multiple_of(g * 8, 8), 8)
        live = local[pl.ds(32 * g + 3, 8, stride=4), :] > 0.0
        over = 1.0 / mass[rows, :]
        for comp in range(4):
            at = pl.ds(32 * g + comp, 8, stride=4)
            force = total[at, :] + total_b[at, :]
            field[comp, rows, :] = jnp.where(live, far[comp, rows, :] + force * over, 0.0)
        return carry

    lax.fori_loop(0, NBLK // 8, group, 0)


def vmem():
    return pl.BlockSpec(memory_space=pltpu.VMEM)


def smem():
    return pl.BlockSpec(memory_space=pltpu.SMEM)


def params(mebibytes=8):
    return pltpu.CompilerParams(vmem_limit_bytes=mebibytes << 20)


def near_scratch():
    return [
        pltpu.VMEM((CHUNKS, 128, LANES), F32),
        pltpu.VMEM((8 * POOL, LANES), F32),
        pltpu.VMEM((8 * POOL, LANES), F32),
        pltpu.VMEM((8 * (COLUMNS + 8), LANES), F32),
        pltpu.VMEM((NBLK, 64, 8, LANES), F32),
        pltpu.VMEM((64, 8, LANES), F32),
    ]


def pack_sources(meta, local, inbound):
    return pl.pallas_call(
        pack_kernel,
        out_shape=shaped(4 * COLUMNS, LANES),
        in_specs=[smem(), vmem(), vmem()],
        out_specs=vmem(),
        scratch_shapes=[pltpu.VMEM((8 * POOL, LANES), F32)]
        + [pltpu.VMEM((8 * (COLUMNS + 8), LANES), F32)] * 2,
        compiler_params=params(20),
        cost_estimate=costs(10),
        name="pack",
    )(meta, local, inbound)


def near_field(meta, counts, turned, strips):
    return pl.pallas_call(
        near_kernel,
        out_shape=(shaped(4 * NBLK, LANES), shaped(4 * INBOUND, LANES)),
        in_specs=[smem(), smem(), vmem(), vmem()],
        out_specs=(vmem(), vmem()),
        scratch_shapes=near_scratch(),
        compiler_params=params(50),
        cost_estimate=costs(60),
        name="near",
    )(meta, counts, turned, strips)


def costs(microseconds):
    return pl.CostEstimate(
        flops=int(microseconds * 1.15e9), bytes_accessed=1 << 20, transcendentals=0
    )


def shaped(*dims, dtype=F32):
    return jax.ShapeDtypeStruct(dims, dtype)


def body(
    positions, masses, counts, export_block, export_dest, near_pairs,
    node_of_block, far_nodes, far_offset, node_centers, m2l_ops,
):
    counts_row = counts.reshape(1, NBLK)
    local, outgoing, slots = pl.pallas_call(
        export_kernel,
        out_shape=(
            shaped(4 * NBLK, LANES), shaped(4 * INBOUND, LANES), shaped(NROWS, dtype=I32),
        ),
        in_specs=[smem()] * 2 + [vmem()] * 3,
        out_specs=(vmem(), vmem(), smem()),
        scratch_shapes=[pltpu.SMEM((NDEV,), I32)],
        compiler_params=params(58),
        cost_estimate=costs(4),
        name="export",
    )(export_block, export_dest.reshape(NROWS), positions, masses, counts_row)
    inbound = lax.all_to_all(
        outgoing.reshape(NDEV, 4 * SLOTS, LANES), AXES, split_axis=0, concat_axis=0, tiled=True
    ).reshape(4 * INBOUND, LANES)
    own_half, other_half, offsets, turned = pl.pallas_call(
        moment_kernel,
        out_shape=(
            shaped(HALF, LANES), shaped(HALF, LANES), shaped(3, NBLK, LANES),
            shaped(NBLK // 8, LANES, LANES, dtype=jnp.bfloat16),
        ),
        in_specs=[smem()] + [vmem()] * 4,
        out_specs=(vmem(), vmem(), vmem(), vmem()),
        scratch_shapes=[pltpu.VMEM((NBLK, LANES), F32), pltpu.VMEM((NNODE, LANES), F32)],
        compiler_params=params(58),
        cost_estimate=costs(8),
        name="moment",
    )(node_of_block, positions, local, node_of_block.reshape(1, NBLK), node_centers)
    chip = [(i, i ^ 1) for i in range(lax.axis_size("dom"))]
    share = own_half + lax.ppermute(other_half, "dom", chip)
    share, inbound = lax.optimization_barrier((share, inbound))
    sub_size = lax.axis_size("sub")
    cores = [[i for i in range(NDEV) if i // sub_size % 2 == core] for core in range(2)]
    spread = (NDEV // 2, 2 * HALF // NDEV, LANES)
    shares = lax.all_to_all(
        share.reshape(spread), AXES, 0, 0, tiled=True, axis_index_groups=cores
    )
    meta = pl.pallas_call(
        build_kernel,
        out_shape=shaped(8, NPAIRS, dtype=I32),
        in_specs=[vmem()] * 3,
        out_specs=vmem(),
        compiler_params=params(),
        cost_estimate=costs(4),
        name="build",
    )(inbound, counts_row, jnp.transpose(near_pairs))
    strips = pack_sources(meta, local, inbound)
    shares, strips = lax.optimization_barrier((shares, strips))
    own_moments = lax.all_to_all(
        jnp.broadcast_to(jnp.sum(shares, 0)[None], spread),
        AXES, 0, 0, tiled=True, axis_index_groups=cores,
    ).reshape(HALF, LANES)
    near_local, near_inbound = near_field(meta, counts, turned, strips)
    own_moments, near_inbound = lax.optimization_barrier((own_moments, near_inbound))
    other_moments = lax.ppermute(own_moments, "dom", chip)
    returned = lax.all_to_all(
        near_inbound.reshape(NDEV, 4 * SLOTS, LANES), AXES, split_axis=0, concat_axis=0, tiled=True
    ).reshape(4 * INBOUND, LANES)
    far = pl.pallas_call(
        far_kernel,
        out_shape=shaped(4, NBLK, LANES),
        in_specs=[smem(), smem()] + [vmem()] * 4,
        out_specs=vmem(),
        scratch_shapes=[pltpu.VMEM((NNODE, LANES), F32)] * 2,
        compiler_params=params(),
        cost_estimate=costs(13),
        name="far",
    )(
        jnp.transpose(far_nodes), jnp.transpose(far_offset), own_moments, other_moments,
        jnp.transpose(m2l_ops, (1, 0, 2)).reshape(NCOEF * NOFF, NCOEF), offsets,
    )
    return pl.pallas_call(
        join_kernel,
        out_shape=shaped(4, NBLK, LANES),
        in_specs=[smem(), smem()] + [vmem()] * 5,
        out_specs=vmem(),
        scratch_shapes=[pltpu.VMEM((4 * NBLK, LANES), F32)] * 2,
        compiler_params=params(),
        cost_estimate=costs(4),
        name="join",
    )(export_block, slots, near_local, returned, far, local, masses)


def solution(mesh):
    both = ("dom", "sub")
    placed = (
        P(None, both, None), P(both, None), P(both), P(both), P(both, None), P(both, None),
        P(both), P(both, None), P(both, None), P(), P(),
    )
    return jax.shard_map(
        body, mesh=mesh, in_specs=placed, out_specs=P(None, both, None), check_vma=False
    )
```

```python
import jax
import jax.numpy as jnp
import numpy as np
from jax import lax
from jax.experimental import pallas as pl
from jax.experimental.pallas import tpu as pltpu
from jax.sharding import PartitionSpec as P

SOFTENING = 0.0025
LANES = 128
NBLK = 128
NDEV = 128
SLOTS = 4
NNODE = 2048
HALF = NNODE // 2
NROWS = 256
NPAIRS = 1024
NFAR = 32
NOFF = 16
NCOEF = 84
INBOUND = NDEV * SLOTS
POOL = NBLK + INBOUND
NBUCKET = 16
AXES = ("dom", "sub")
F32 = jnp.float32
I32 = jnp.int32


def exponent_table():
    triples = []
    for degree in range(7):
        for first in range(degree, -1, -1):
            for second in range(degree - first, -1, -1):
                triples.append((first, second, degree - first - second))
    return triples


TRIPLES = exponent_table()
PLACE = {triple: place for place, triple in enumerate(TRIPLES)}


def monomial_chain(root, x, y, z):
    terms = []
    for a, b, c in TRIPLES:
        if a > 0:
            lower, axis = (a - 1, b, c), x
        elif b > 0:
            lower, axis = (a, b - 1, c), y
        elif c > 0:
            lower, axis = (a, b, c - 1), z
        else:
            terms.append(root)
            continue
        parent = terms[PLACE[lower]]
        terms.append(axis if parent is None else parent * axis)
    return terms


def own_flip():
    return lax.bitwise_and(lax.axis_index("dom"), 1) * HALF


def export_kernel(block_s, dest_s, pos, mass, counts, local, outgoing, slots, used):
    lane = lax.broadcasted_iota(I32, (8, LANES), 1)
    sub = lax.broadcasted_iota(I32, (8, LANES), 0)
    counts_row = counts[...].astype(F32)
    for g in range(NBLK // 8):
        rows = slice(8 * g, 8 * g + 8)
        count_col = jnp.sum(jnp.where(lane == sub + 8 * g, counts_row, 0.0), 1, keepdims=True)
        weight = jnp.where(lane.astype(F32) < count_col, mass[rows, :], 0.0)
        for axis in range(3):
            local[pl.ds(32 * g + axis, 8, stride=4), :] = pos[axis, rows, :]
        local[pl.ds(32 * g + 3, 8, stride=4), :] = weight
    outgoing[...] = jnp.zeros_like(outgoing)

    def clear(i, carry):
        used[i] = 0
        return carry

    lax.fori_loop(0, NDEV, clear, 0, unroll=8)

    def place(r, carry):
        d = dest_s[r]
        k = used[d]
        used[d] = k + 1
        s = d * SLOTS + k
        slots[r] = s
        outgoing[pl.ds(4 * s, 4), :] = local[pl.ds(4 * block_s[r], 4), :]
        return carry

    lax.fori_loop(0, NROWS, place, 0, unroll=16)


def moment_kernel(
    node_s, pos, local, nodes, centers, own_half, other_half, offsets, turned, mom, partial
):
    for c in range(NBLK // 8):
        whole = local[32 * c : 32 * c + 32, :]
        high = whole.astype(jnp.bfloat16).astype(F32)
        rest = whole - high
        middle = rest.astype(jnp.bfloat16).astype(F32)
        stack = [high, middle, rest - middle, jnp.zeros((32, LANES), F32)]
        turned[c] = jnp.concatenate(stack, 0).T.astype(jnp.bfloat16)
    lane = lax.broadcasted_iota(I32, (8, LANES), 1)
    sub = lax.broadcasted_iota(I32, (8, LANES), 0)
    wide = lax.broadcasted_iota(I32, (8, NNODE), 1).astype(F32)
    nodes_row = nodes[...].astype(F32)

    def group(g, carry):
        rows = pl.ds(pl.multiple_of(g * 8, 8), 8)
        diag = lane == sub + 8 * g
        node_col = jnp.sum(jnp.where(diag, nodes_row, 0.0), 1, keepdims=True)
        weight = local[pl.ds(32 * g + 3, 8, stride=4), :]
        picked = wide == node_col
        rel = []
        for axis in range(3):
            center = jnp.sum(
                jnp.where(picked, centers[axis : axis + 1, :], 0.0), 1, keepdims=True
            )
            rel.append(pos[axis, rows, :] - center)
            offsets[axis, rows, :] = rel[axis]
        terms = monomial_chain(weight, *rel)
        total = jnp.zeros((8, LANES), F32)
        for k in range(NCOEF):
            total = jnp.where(lane == k, jnp.sum(terms[k], 1, keepdims=True), total)
        mom[rows, :] = total
        return carry

    lax.fori_loop(0, NBLK // 8, group, 0)
    partial[...] = jnp.zeros_like(partial)

    def bin_block(b, carry):
        n = lax.bitwise_xor(node_s[b], flip)
        partial[pl.ds(n, 1), :] = partial[pl.ds(n, 1), :] + mom[pl.ds(b, 1), :]
        return carry

    flip = own_flip()
    lax.fori_loop(0, NBLK, bin_block, 0, unroll=8)
    own_half[...] = partial[pl.ds(0, HALF), :]
    other_half[...] = partial[pl.ds(HALF, HALF), :]


CHUNKS = NBLK // 32
BATCH = 64
WIDE = 4
COLUMNS = NPAIRS + NBLK


def build_kernel(inbound, counts, pairs, meta):
    wide_sub = lax.broadcasted_iota(I32, (8, NPAIRS), 0)
    square_lane = lax.broadcasted_iota(I32, (LANES, LANES), 1)
    square_sub = lax.broadcasted_iota(I32, (LANES, LANES), 0)
    lane = lax.broadcasted_iota(I32, (8, LANES), 1)
    sub = lax.broadcasted_iota(I32, (8, LANES), 0)
    counts_row = counts[...].astype(F32)
    target = pairs[0:1, :]
    source = pairs[1:2, :]

    def received(g, total):
        weight = inbound[pl.ds(32 * g + 3, 8, stride=4), :]
        col = jnp.sum(jnp.where(weight > 0.0, 1.0, 0.0), 1, keepdims=True)
        return total + jnp.where(wide_sub + 8 * g + NBLK == source, col, 0.0)

    live = lax.fori_loop(0, INBOUND // 8, received, jnp.zeros((8, NPAIRS), F32), unroll=8)
    for g in range(NBLK // 8):
        col = jnp.sum(jnp.where(lane == sub + 8 * g, counts_row, 0.0), 1, keepdims=True)
        live = live + jnp.where(wide_sub + 8 * g == source, col, 0.0)
    live = jnp.sum(live, 0, keepdims=True)
    totals = jnp.zeros((LANES, LANES), F32)
    for c in range(NPAIRS // LANES):
        at = slice(c * LANES, (c + 1) * LANES)
        totals = totals + jnp.where(square_sub == target[:, at], live[:, at], 0.0)
    totals = jnp.sum(totals, 1, keepdims=True)
    columns = jnp.floor((totals + (LANES - 1)) * (1.0 / LANES))
    diag = square_lane == square_sub
    columns_row = jnp.sum(jnp.where(diag, columns, 0.0), 0, keepdims=True)
    starts = jnp.sum(jnp.where(square_lane < square_sub, columns_row, 0.0), 1, keepdims=True)
    starts_row = jnp.sum(jnp.where(diag, starts, 0.0), 0, keepdims=True)
    upper = (square_sub < square_lane).astype(F32)
    running = starts * LANES
    for c in range(NPAIRS // LANES):
        at = slice(c * LANES, (c + 1) * LANES)
        hit = (square_sub == target[:, at]).astype(F32)
        held = hit * live[:, at]
        ahead = jnp.dot(held, upper, preferred_element_type=F32) + running
        meta[0:1, at] = jnp.sum(hit * ahead, 0, keepdims=True).astype(I32)
        running = running + jnp.sum(held, 1, keepdims=True)
    meta[1:2, :] = source * 256 + live.astype(I32)
    meta[2:8, :] = jnp.zeros((6, NPAIRS), I32)
    meta[2:3, 0:LANES] = starts_row.astype(I32)
    meta[3:4, 0:LANES] = columns_row.astype(I32)


def pack_kernel(meta, local, inbound, packed, pool, strips, strips_b):
    lane = lax.broadcasted_iota(I32, (8, LANES), 1)
    upper = lax.broadcasted_iota(I32, (8, LANES), 0) >= 4

    def double(b, offset, blocks):
        two = blocks[pl.ds(pl.multiple_of(8 * b, 8), 8), :]
        turn = pltpu.roll(two, 4, 0)
        at = pl.multiple_of(16 * b + offset, 16)
        pool[pl.ds(at, 8), :] = jnp.where(upper, turn, two)
        pool[pl.ds(at + 8, 8), :] = jnp.where(upper, two, turn)

    def double_local(b, carry):
        double(b, 0, local)
        return carry

    def double_inbound(b, carry):
        double(b, 8 * NBLK, inbound)
        return carry

    lax.fori_loop(0, NBLK // 2, double_local, 0, unroll=8)
    lax.fori_loop(0, INBOUND // 2, double_inbound, 0, unroll=8)

    def clear(c, carry):
        strips[pl.ds(pl.multiple_of(c * 64, 64), 64), :] = jnp.zeros((64, LANES), F32)
        strips_b[pl.ds(pl.multiple_of(c * 64, 64), 64), :] = jnp.zeros((64, LANES), F32)
        return carry

    lax.fori_loop(0, (COLUMNS + 8) // 8, clear, 0)

    def pack(i, carry):
        ready = []
        for u in range(BATCH):
            where = meta[0, i * BATCH + u]
            what = meta[1, i * BATCH + u]
            first = lax.bitwise_and(where, LANES - 1)
            column = lax.shift_right_logical(where, 7) + 1
            block = lax.shift_right_logical(what, 8)
            last = first + lax.bitwise_and(what, 255)
            tile = pltpu.roll(pool[pl.ds(pl.multiple_of(8 * block, 8), 8), :], first, 1)
            keep = jnp.logical_and(place >= first, place < last)
            ready.append((column, jnp.where(keep, tile, 0.0)))
        for u, (column, tile) in enumerate(ready):
            at = pl.ds(pl.multiple_of(8 * column, 8), 8)
            held = (strips, strips_b)[u % 2]
            held[at, :] = held[at, :] + tile
        return carry

    place = jnp.where(upper, lane + LANES, lane)
    lax.fori_loop(0, NPAIRS // BATCH, pack, 0)

    def merge(g, carry):
        at = pl.multiple_of(32 * g, 32)
        before = strips[pl.ds(at, 8), :] + strips_b[pl.ds(at, 8), :]
        before = pltpu.roll(before, 4, 0)
        for u in (1, 3):
            one = strips[pl.ds(at + 8 * u, 8), :] + strips_b[pl.ds(at + 8 * u, 8), :]
            two = strips[pl.ds(at + 8 * u + 8, 8), :] + strips_b[pl.ds(at + 8 * u + 8, 8), :]
            after = pltpu.roll(two, 4, 0)
            packed[pl.ds(pl.multiple_of(16 * g + 4 * u - 4, 8), 8), :] = jnp.where(
                upper, after, one
            ) + jnp.where(upper, one, before)
            before = after
        return carry

    lax.fori_loop(0, COLUMNS // 4, merge, 0, unroll=4)


def near_kernel(
    meta, counts, turned, strips, near_local, near_inbound,
    acc_t, acc, acc_b, results, rows_s, sums_s,
):
    nothing = jnp.zeros((8, LANES), F32)
    lane = lax.broadcasted_iota(I32, (8, LANES), 1)
    sub = lax.broadcasted_iota(I32, (8, LANES), 0)
    upper = sub >= 4

    def clear(b, carry):
        at = pl.ds(pl.multiple_of(b * 128, 128), 128)
        for held in (acc, acc_b):
            held[at, :] = jnp.zeros((128, LANES), F32)
        return carry

    lax.fori_loop(0, 8 * POOL // 128, clear, 0)
    place = jnp.where(upper, lane + LANES, lane)

    for c in range(CHUNKS):
        acc_t[c] = jnp.zeros((128, LANES), F32)
    part_row = lax.bitwise_and(lax.broadcasted_iota(I32, (LANES, 4 * LANES), 0), 31)
    part_comp = lax.shift_right_logical(lax.broadcasted_iota(I32, (LANES, 4 * LANES), 1), 7)

    def spread(i, carry):
        pick = (part_row == 4 * i + part_comp).astype(F32).astype(jnp.bfloat16)
        for c in range(NBLK // 8):
            wide = jnp.dot(turned[c], pick, preferred_element_type=F32)
            for k in range(16):
                for comp in range(4):
                    rows_s[8 * c + i, 4 * k + comp] = wide[
                        8 * k : 8 * k + 8, LANES * comp : LANES * comp + LANES
                    ]
        return carry

    lax.fori_loop(0, 8, spread, 0)

    def lanes_of(t):
        first = lax.bitwise_and(t, 31) * 4
        return lax.shift_right_logical(t, 5), [
            jnp.zeros((8, LANES), I32) + (first + comp) for comp in range(4)
        ]

    low = [lax.bitwise_and(sub, bit) == 0 for bit in (1, 2, 4)]

    def fold(tiles):
        for place, bit in ((2, 4), (1, 2), (0, 1)):
            tiles = [
                jnp.where(low[place], tiles[i], tiles[i + bit])
                + jnp.where(
                    low[place],
                    pltpu.roll(tiles[i], 8 - bit, 0),
                    pltpu.roll(tiles[i + bit], bit, 0),
                )
                for i in range(bit)
            ]
        return tiles[0]

    def run(level, t):
        base = meta[2, t]
        count = meta[3, t]
        chunk, picks = lanes_of(t)
        for j in range(4 * level):
            sums_s[j] = nothing

        def columns(at, gang):
            cols, sums = [], []
            for u in range(gang):
                cols.append(
                    [
                        jnp.broadcast_to(strips[pl.ds(4 * (at + u) + comp, 1), :], (8, LANES))
                        for comp in range(4)
                    ]
                )
                sums.append([nothing] * 4)
            for k in range(level):
                rows = [rows_s[t, 4 * k + comp] for comp in range(4)]
                across = [sums_s[4 * k + comp] for comp in range(4)]
                for u in range(gang):
                    delta = [cols[u][axis] - rows[axis] for axis in range(3)]
                    dist2 = (
                        delta[0] * delta[0] + delta[1] * delta[1]
                        + (delta[2] * delta[2] + SOFTENING)
                    )
                    inverse = lax.rsqrt(dist2)
                    pot = cols[u][3] * rows[3] * inverse
                    cube = pot * (inverse * inverse)
                    parts = [pot] + [cube * delta[axis] for axis in range(3)]
                    sums[u] = [old + part for old, part in zip(sums[u], parts)]
                    across = [old + part for old, part in zip(across, parts)]
                for comp in range(4):
                    sums_s[4 * k + comp] = across[comp]
            for u in range(0, gang, 2):
                both = fold(sums[u] + sums[min(u + 1, gang - 1)])
                swapped = pltpu.roll(both, 4, 0)
                here = pl.multiple_of(8 * (at + u) + 8, 8)
                results[pl.ds(here, 8), :] = both
                results[pl.ds(here - 4, 4), :] = swapped[4:8, :]
                if gang > 1:
                    results[pl.ds(here + 8, 4), :] = swapped[0:4, :]

        def step(i, carry):
            columns(base + WIDE * i, WIDE)
            return carry

        lax.fori_loop(0, lax.div(count, WIDE), step, 0)
        size = WIDE // 2
        while size > 0:
            done = base + lax.bitwise_and(count, -2 * size)
            pl.when(lax.bitwise_and(count, size) > 0)(
                lambda done=done, size=size: columns(done, size)
            )
            size //= 2
        for k in range(level):
            res = acc_t[chunk, 8 * k : 8 * k + 8, :]
            for comp in range(4):
                whole = jnp.sum(sums_s[4 * k + comp], 1, keepdims=True)
                res = jnp.where(lane == picks[comp], whole, res)
            acc_t[chunk, 8 * k : 8 * k + 8, :] = res

    def per_target(t, carry):
        level = lax.shift_right_logical(counts[t] - 1, 3)

        def choose(least, most):
            if least == most:
                run(least + 1, t)
                return
            middle = (least + most + 1) // 2
            pl.when(level < middle)(lambda: choose(least, middle - 1))
            pl.when(level >= middle)(lambda: choose(middle, most))

        choose(0, NBUCKET - 1)
        return carry

    lax.fori_loop(0, NBLK, per_target, 0)

    def unpack(i, carry):
        ready = []
        for u in range(BATCH):
            where = meta[0, i * BATCH + u]
            what = meta[1, i * BATCH + u]
            first = lax.bitwise_and(where, LANES - 1)
            column = lax.shift_right_logical(where, 7) + 1
            block = lax.shift_right_logical(what, 8)
            last = first + lax.bitwise_and(what, 255)
            tile = results[pl.ds(pl.multiple_of(8 * column, 8), 8), :]
            keep = jnp.logical_and(place >= first, place < last)
            tile = jnp.where(keep, tile, 0.0)
            ready.append((block, pltpu.roll(tile, lax.bitwise_and(LANES - first, LANES - 1), 1)))
        for u, (block, tile) in enumerate(ready):
            at = pl.ds(pl.multiple_of(8 * block, 8), 8)
            held = (acc, acc_b)[u % 2]
            held[at, :] = held[at, :] + tile
        return carry

    lax.fori_loop(0, NPAIRS // BATCH, unpack, 0)

    sign = jnp.where(lax.bitwise_and(sub, 3) == 0, -1.0, 1.0)

    def joined(at):
        one, two = (
            acc[pl.ds(here, 8), :] + acc_b[pl.ds(here, 8), :]
            for here in (at, at + 8)
        )
        one = one + pltpu.roll(one, 4, 0)
        two = two + pltpu.roll(two, 4, 0)
        return jnp.where(upper, two, one)

    for c in range(CHUNKS):
        back = acc_t[c].T
        for g in range(16):
            both = back[8 * g : 8 * g + 8, :] * sign - joined(c * 256 + 16 * g)
            near_local[c * 128 + 8 * g : c * 128 + 8 * g + 8, :] = both

    def finish(g, carry):
        at = pl.multiple_of(g * 16, 16)
        near_inbound[pl.ds(pl.multiple_of(g * 8, 8), 8), :] = -joined(NBLK * 8 + at)
        return carry

    lax.fori_loop(0, INBOUND // 2, finish, 0, unroll=8)


def far_kernel(
    far_nodes, far_offset, own_half, other_half, ops, offsets, far, binned, moments
):
    moments[pl.ds(0, HALF), :] = own_half[...]
    moments[pl.ds(HALF, HALF), :] = other_half[...]
    flip = own_flip()
    which = lax.broadcasted_iota(I32, (NOFF, LANES), 0)

    def gather(b, carry):
        total = jnp.zeros((NOFF, LANES), F32)
        for j in range(NFAR):
            node = lax.bitwise_xor(far_nodes[j, b], flip)
            row = jnp.broadcast_to(moments[pl.ds(node, 1), :], (NOFF, LANES))
            total = total + jnp.where(which == far_offset[j, b], row, 0.0)
        binned[pl.ds(pl.multiple_of(b * NOFF, NOFF), NOFF), :] = total
        return carry

    lax.fori_loop(0, NBLK, gather, 0, unroll=2)
    series = jnp.zeros((NBLK, NCOEF), F32)
    for o in range(NOFF):
        series = series + lax.dot_general(
            binned[pl.ds(o, NBLK, stride=NOFF), :][:, :NCOEF],
            ops[pl.ds(o, NCOEF, stride=NOFF), :],
            (((1,), (1,)), ((), ())),
            precision=lax.Precision.HIGHEST,
            preferred_element_type=F32,
        )
    binned[pl.ds(0, NBLK), pl.ds(0, NCOEF)] = series

    def group(g, carry):
        rows = pl.ds(pl.multiple_of(g * 8, 8), 8)
        x, y, z = (offsets[axis, rows, :] for axis in range(3))
        coefs = binned[rows, :]
        terms = monomial_chain(None, x, y, z)
        terms[0] = jnp.ones((8, LANES), F32)
        total = [jnp.zeros((8, LANES), F32) for comp in range(4)]
        for k, triple in enumerate(TRIPLES):
            coef = jnp.broadcast_to(coefs[:, k : k + 1], (8, LANES))
            total[0] = total[0] + (coef if k == 0 else coef * terms[k])
            for axis in range(3):
                power = triple[axis]
                if power > 0:
                    lower = list(triple)
                    lower[axis] -= 1
                    place = PLACE[tuple(lower)]
                    slope = coef if power == 1 else coef * float(power)
                    if place > 0:
                        slope = slope * terms[place]
                    total[axis + 1] = total[axis + 1] - slope
        for comp in range(4):
            far[comp, rows, :] = total[comp]
        return carry

    lax.fori_loop(0, NBLK // 8, group, 0)


def join_kernel(block_s, slots, near, returned, far, local, mass, field, total, total_b):
    total[...] = near[...]
    total_b[...] = jnp.zeros_like(total_b)

    def back(i, carry):
        ready = [returned[pl.ds(4 * slots[8 * i + u], 4), :] for u in range(8)]
        for u in range(8):
            at = pl.ds(4 * block_s[8 * i + u], 4)
            held = (total, total_b)[u % 2]
            held[at, :] = held[at, :] + ready[u]
        return carry

    lax.fori_loop(0, NROWS // 8, back, 0)

    def group(g, carry):
        rows = pl.ds(pl.multiple_of(g * 8, 8), 8)
        live = local[pl.ds(32 * g + 3, 8, stride=4), :] > 0.0
        over = 1.0 / mass[rows, :]
        for comp in range(4):
            at = pl.ds(32 * g + comp, 8, stride=4)
            force = total[at, :] + total_b[at, :]
            field[comp, rows, :] = jnp.where(live, far[comp, rows, :] + force * over, 0.0)
        return carry

    lax.fori_loop(0, NBLK // 8, group, 0)


def vmem():
    return pl.BlockSpec(memory_space=pltpu.VMEM)


def smem():
    return pl.BlockSpec(memory_space=pltpu.SMEM)


def params(mebibytes=8):
    return pltpu.CompilerParams(vmem_limit_bytes=mebibytes << 20)


def near_scratch():
    return [
        pltpu.VMEM((CHUNKS, 128, LANES), F32),
        pltpu.VMEM((8 * POOL, LANES), F32),
        pltpu.VMEM((8 * POOL, LANES), F32),
        pltpu.VMEM((8 * (COLUMNS + 8), LANES), F32),
        pltpu.VMEM((NBLK, 64, 8, LANES), F32),
        pltpu.VMEM((64, 8, LANES), F32),
    ]


def pack_sources(meta, local, inbound):
    return pl.pallas_call(
        pack_kernel,
        out_shape=shaped(4 * COLUMNS, LANES),
        in_specs=[smem(), vmem(), vmem()],
        out_specs=vmem(),
        scratch_shapes=[pltpu.VMEM((8 * POOL, LANES), F32)]
        + [pltpu.VMEM((8 * (COLUMNS + 8), LANES), F32)] * 2,
        compiler_params=params(20),
        cost_estimate=costs(10),
        name="pack",
    )(meta, local, inbound)


def near_field(meta, counts, turned, strips):
    return pl.pallas_call(
        near_kernel,
        out_shape=(shaped(4 * NBLK, LANES), shaped(4 * INBOUND, LANES)),
        in_specs=[smem(), smem(), vmem(), vmem()],
        out_specs=(vmem(), vmem()),
        scratch_shapes=near_scratch(),
        compiler_params=params(50),
        cost_estimate=costs(60),
        name="near",
    )(meta, counts, turned, strips)


def costs(microseconds):
    return pl.CostEstimate(
        flops=int(microseconds * 1.15e9), bytes_accessed=1 << 20, transcendentals=0
    )


def shaped(*dims, dtype=F32):
    return jax.ShapeDtypeStruct(dims, dtype)


def body(
    positions, masses, counts, export_block, export_dest, near_pairs,
    node_of_block, far_nodes, far_offset, node_centers, m2l_ops,
):
    counts_row = counts.reshape(1, NBLK)
    local, outgoing, slots = pl.pallas_call(
        export_kernel,
        out_shape=(
            shaped(4 * NBLK, LANES), shaped(4 * INBOUND, LANES), shaped(NROWS, dtype=I32),
        ),
        in_specs=[smem()] * 2 + [vmem()] * 3,
        out_specs=(vmem(), vmem(), smem()),
        scratch_shapes=[pltpu.SMEM((NDEV,), I32)],
        compiler_params=params(58),
        cost_estimate=costs(4),
        name="export",
    )(export_block, export_dest.reshape(NROWS), positions, masses, counts_row)
    inbound = lax.all_to_all(
        outgoing.reshape(NDEV, 4 * SLOTS, LANES), AXES, split_axis=0, concat_axis=0, tiled=True
    ).reshape(4 * INBOUND, LANES)
    own_half, other_half, offsets, turned = pl.pallas_call(
        moment_kernel,
        out_shape=(
            shaped(HALF, LANES), shaped(HALF, LANES), shaped(3, NBLK, LANES),
            shaped(NBLK // 8, LANES, LANES, dtype=jnp.bfloat16),
        ),
        in_specs=[smem()] + [vmem()] * 4,
        out_specs=(vmem(), vmem(), vmem(), vmem()),
        scratch_shapes=[pltpu.VMEM((NBLK, LANES), F32), pltpu.VMEM((NNODE, LANES), F32)],
        compiler_params=params(58),
        cost_estimate=costs(8),
        name="moment",
    )(node_of_block, positions, local, node_of_block.reshape(1, NBLK), node_centers)
    chip = [(i, i ^ 1) for i in range(lax.axis_size("dom"))]
    share = own_half + lax.ppermute(other_half, "dom", chip)
    share, inbound = lax.optimization_barrier((share, inbound))
    sub_size = lax.axis_size("sub")
    cores = [[i for i in range(NDEV) if i // sub_size % 2 == core] for core in range(2)]
    spread = (NDEV // 2, 2 * HALF // NDEV, LANES)
    shares = lax.all_to_all(
        share.reshape(spread), AXES, 0, 0, tiled=True, axis_index_groups=cores
    )
    meta = pl.pallas_call(
        build_kernel,
        out_shape=shaped(8, NPAIRS, dtype=I32),
        in_specs=[vmem()] * 3,
        out_specs=vmem(),
        compiler_params=params(),
        cost_estimate=costs(4),
        name="build",
    )(inbound, counts_row, jnp.transpose(near_pairs))
    strips = pack_sources(meta, local, inbound)
    shares, strips = lax.optimization_barrier((shares, strips))
    own_moments = lax.all_to_all(
        jnp.broadcast_to(jnp.sum(shares, 0)[None], spread),
        AXES, 0, 0, tiled=True, axis_index_groups=cores,
    ).reshape(HALF, LANES)
    near_local, near_inbound = near_field(meta, counts, turned, strips)
    own_moments, near_inbound = lax.optimization_barrier((own_moments, near_inbound))
    other_moments = lax.ppermute(own_moments, "dom", chip)
    returned = lax.all_to_all(
        near_inbound.reshape(NDEV, 4 * SLOTS, LANES), AXES, split_axis=0, concat_axis=0, tiled=True
    ).reshape(4 * INBOUND, LANES)
    far = pl.pallas_call(
        far_kernel,
        out_shape=shaped(4, NBLK, LANES),
        in_specs=[smem(), smem()] + [vmem()] * 4,
        out_specs=vmem(),
        scratch_shapes=[pltpu.VMEM((NNODE, LANES), F32)] * 2,
        compiler_params=params(),
        cost_estimate=costs(13),
        name="far",
    )(
        jnp.transpose(far_nodes), jnp.transpose(far_offset), own_moments, other_moments,
        jnp.transpose(m2l_ops, (1, 0, 2)).reshape(NCOEF * NOFF, NCOEF), offsets,
    )
    return pl.pallas_call(
        join_kernel,
        out_shape=shaped(4, NBLK, LANES),
        in_specs=[smem(), smem()] + [vmem()] * 5,
        out_specs=vmem(),
        scratch_shapes=[pltpu.VMEM((4 * NBLK, LANES), F32)] * 2,
        compiler_params=params(),
        cost_estimate=costs(4),
        name="join",
    )(export_block, slots, near_local, returned, far, local, masses)


def solution(mesh):
    both = ("dom", "sub")
    placed = (
        P(None, both, None), P(both, None), P(both), P(both), P(both, None), P(both, None),
        P(both), P(both, None), P(both, None), P(), P(),
    )
    return jax.shard_map(
        body, mesh=mesh, in_specs=placed, out_specs=P(None, both, None), check_vma=False
    )
```
